32 devices in a mesh: parts: 2 (over y), replica: 4 (over x, core), tensor: 4 (over z).
Axes of the slice: x: 2, y: 2, z: 4, core: 2. Of those that a mesh axis runs over, the one named last changes fastest.
Arguments:
- hidden: bfloat16 [112, 2, 8192], P(('parts', 'replica'), None, 'tensor'), parts along dimension 0, may hold values from -6 to 6
- queries: bfloat16 [112, 2, 64, 128], P(('parts', 'replica'), None, 'tensor'), parts along dimension 0, may hold values from -220 to 220
- kv_cache: bfloat16 [96, 128, 8, 256], P(('parts', 'replica'), None, 'tensor'), parts along dimension 0, may hold values from -6.5 to 6.5
- w_kv: bfloat16 [8192, 8, 256], P(None, 'tensor'), may hold values from -0.0625 to 0.0625
- store_a: bfloat16 [64, 2, 64, 8192], P(('parts', 'replica'), None, None, 'tensor'), parts along dimension 0, may hold values from -0.0625 to 0.0625
- store_b: bfloat16 [64, 2, 64, 1024], P(('parts', 'replica'), None, None, 'tensor'), parts along dimension 0, may hold values from -0.75 to 0.75
- lengths: int32 [96], P('parts'), parts along dimension 0, may hold values from 2 to 128, as said below
- arrival_from: int32 [8, 2], P('parts'), parts along dimension 0, may hold values from 0 to 3, as said below
- arrival_slot: int32 [8, 2], P('parts'), parts along dimension 0, may hold values from 0 to 11, as said below
- resident_adapter: int32 [96], P('parts'), parts along dimension 0, may hold values from 0 to 7
- arrival_adapter: int32 [8, 2], P('parts'), parts along dimension 0, may hold values from 0 to 3
- hot_holder: int32 [32], P('parts'), parts along dimension 0, may hold values from 0 to 31, as said below
- hot_dest: int32 [32, 1], P('parts'), parts along dimension 0, may hold values from 0 to 3, as said below
Outputs:
- attn_out: bfloat16 [112, 2, 8192], P(('parts', 'replica'), None, 'tensor'), parts along dimension 0
- new_kv: bfloat16 [112, 2, 8, 256], P(('parts', 'replica'), None, 'tensor'), parts along dimension 0
- arrival_cache: bfloat16 [16, 128, 8, 256], P(('parts', 'replica'), None, 'tensor'), parts along dimension 0
- installed_a: bfloat16 [32, 2, 64, 8192], P(('parts', 'replica'), None, None, 'tensor'), parts along dimension 0
- installed_b: bfloat16 [32, 2, 64, 1024], P(('parts', 'replica'), None, None, 'tensor'), parts along dimension 0
The draws below stay inside these ranges and needn't reach their ends.
There are 2 independent parts, one for each index of `parts`. The reference program is written for one: setup_inputs(seed, part) draws one part's arguments, and reference() takes and returns one part's arrays. A program takes and returns all parts, laid end to end along the dimension named above; an argument that names none is the same for every part. Nothing has to cross between parts.
Inputs may be any that keep to these rules, and one draw needn't show every extreme that they name: `lengths`: every request listed by arrival_from and arrival_slot holds more than 96 rows; some request holds exactly 128. `arrival_from`: row r lists 2 distinct replicas, none equal to r; each replica appears exactly 2 times in the whole array. `arrival_slot`: no request (replica and slot) is listed twice. `hot_holder`: entry h is the holder's replica times 8 plus its slot; the holder's replica is not in row h of hot_dest; the holders of rows c * 4 to c * 4 + 3 lie on distinct replicas. `hot_dest`: for each c below 4, rows c * 4 to c * 4 + 3 together list every replica exactly once.
All inputs are finite; a program needn't handle non-finite values.
Results may differ from the reference program's by a relative error of at most 0.0071.
Values may be sent and summed in bfloat16 or wider, within the bound.
A program may use at most 64 MiB of HBM per device.

```python
import math
import jax
import jax.numpy as jnp
from jax import lax

D = 8192
HEADS = 64
KEY_VALUE_HEADS = 8
HEAD_WIDTH = 128
RANK = 64
NEW_TOKEN_COUNT = 2
COPIES = 4
RES = 12
CAP = 128
ASLOT = 8
ARRIVE = 2
FAN = 1
SPANS = 4
N_REPLICA = 4


def plan_draw(key):
    key_list = jax.random.split(jax.random.fold_in(key, 7), 9)
    shuffle = jax.random.permutation(key_list[0], N_REPLICA).astype(jnp.int32)
    inverse = jnp.argsort(shuffle).astype(jnp.int32)
    offsets = (1 + jax.random.permutation(key_list[1], N_REPLICA - 1)[:ARRIVE]).astype(jnp.int32)
    sender = shuffle[(inverse[:, None] + offsets[None, :]) % N_REPLICA]
    slot_keys = jax.random.split(key_list[2], N_REPLICA)
    slot_orders = jax.vmap(lambda sub_key: jax.random.permutation(sub_key, RES))(slot_keys).astype(jnp.int32)
    top_replica = jax.random.randint(key_list[8], (), 0, N_REPLICA)
    shifted = (slot_orders - slot_orders[:, :1] + (RES - 1)) % RES
    is_top = (jnp.arange(N_REPLICA, dtype=jnp.int32) == top_replica)[:, None]
    slot_orders = jnp.where(is_top, shifted, slot_orders).astype(jnp.int32)
    arrive_ids = jnp.arange(ARRIVE, dtype=jnp.int32)
    source_slot = slot_orders[sender, arrive_ids[None, :]]
    ceilings = jax.random.randint(key_list[3], (N_REPLICA, 1), CAP // 8, CAP + 1)
    length_table = jax.random.randint(key_list[4], (N_REPLICA, RES), 2, ceilings + 1)
    long_lengths = jax.random.randint(key_list[5], (N_REPLICA, ARRIVE), 3 * CAP // 4 + 1, CAP + 1)
    length_table = length_table.at[sender, source_slot].set(long_lengths)
    chosen = jax.random.randint(key_list[6], (), 0, N_REPLICA)
    length_table = length_table.at[sender[chosen, 0], source_slot[chosen, 0]].set(CAP)
    dest_rows = []
    holder_rows = []
    for copy_id in range(COPIES):
        copy_key = jax.random.fold_in(key_list[7], copy_id)
        key_perm, key_pick, key_slot = jax.random.split(copy_key, 3)
        shuffled = jax.random.permutation(key_perm, N_REPLICA).astype(jnp.int32)
        dest_rows.append(shuffled.reshape(SPANS, FAN))
        pick_idx = jax.random.randint(key_pick, (SPANS,), 0, FAN)
        next_span = (jnp.arange(SPANS, dtype=jnp.int32) + 1) % SPANS
        holder_rep = shuffled[next_span * FAN + pick_idx]
        holder_slot = jax.random.randint(key_slot, (SPANS,), 0, ASLOT)
        holder_rows.append(holder_rep * ASLOT + holder_slot)
    hot_dest = jnp.concatenate(dest_rows, axis=0).astype(jnp.int32)
    hot_holder = jnp.concatenate(holder_rows, axis=0).astype(jnp.int32)
    return (length_table.reshape(-1).astype(jnp.int32), sender.astype(jnp.int32), source_slot.astype(jnp.int32), hot_holder, hot_dest)


def cache_draw(key):
    drawn = jax.random.truncated_normal(jax.random.fold_in(key, 21), -6.0, 6.0, (N_REPLICA * RES, CAP, KEY_VALUE_HEADS, 2 * HEAD_WIDTH), jnp.float32)
    drawn = drawn.astype(jnp.bfloat16).astype(jnp.float32)
    return drawn


def draw_kv_cache(key, part):
    return cache_draw(key).astype(jnp.bfloat16)


def draw_queries(key, part):
    request_slot_count = N_REPLICA * (RES + ARRIVE)
    drawn = jax.random.truncated_normal(jax.random.fold_in(key, 31), -6.0, 6.0, (request_slot_count, NEW_TOKEN_COUNT, HEADS, HEAD_WIDTH), jnp.float32)
    return drawn.astype(jnp.bfloat16)


def draw_lengths(key, part):
    return plan_draw(key)[0]


def draw_arrival_from(key, part):
    return plan_draw(key)[1]


def draw_arrival_slot(key, part):
    return plan_draw(key)[2]


def draw_hot_holder(key, part):
    return plan_draw(key)[3]


def draw_hot_dest(key, part):
    return plan_draw(key)[4]


def with_ends(array, stream_key, low, high):
    longest = array.shape.index(max(array.shape))
    spots = []
    for shift in (0, 1):
        where = [jax.random.randint(jax.random.fold_in(stream_key, axis), (), 0, length) for axis, length in enumerate(array.shape)]
        where[longest] = (where[longest] + shift) % array.shape[longest]
        spots.append(tuple(where))
    return array.at[spots[0]].set(low).at[spots[1]].set(high)


def levels(rng, extent, pieces, smallest, largest):
    loudness, own = 1.0, jax.random.fold_in(rng, 6)
    for axis_at, shards_of in pieces:
        heights = jnp.exp(jax.random.uniform(jax.random.fold_in(own, axis_at), (shards_of,), jnp.float32, smallest / len(pieces), largest / len(pieces)))
        loudness = loudness * jnp.repeat(heights, extent[axis_at] // shards_of).reshape([-1 if axis == axis_at else 1 for axis in range(len(extent))])
    return loudness


def noise(own_key, shape, width, limit, pieces=(), kind=jnp.bfloat16):
    result = width * jax.random.normal(own_key, shape, jnp.float32)
    if pieces:
        result = result * levels(own_key, shape, pieces, -0.22, 0.18)
    return jnp.clip(result, -limit, limit).astype(kind)


def setup_inputs(seed: int = 0, part: int = 0) -> dict:
    arg_keys = jax.random.split(jax.random.key(seed), 14)
    own_keys = jax.random.split(jax.random.fold_in(arg_keys[13], part), 14)
    hidden = noise(own_keys[0], (N_REPLICA * (RES + ARRIVE), NEW_TOKEN_COUNT, D), 1.0, 6.0, ((0, 4), (2, 4)))
    queries = draw_queries(jax.random.fold_in(jax.random.fold_in(arg_keys[13], part), 71), part)
    kv_cache = draw_kv_cache(jax.random.fold_in(jax.random.fold_in(arg_keys[13], part), 71), part)
    w_kv = noise(arg_keys[3], (D, KEY_VALUE_HEADS, 2 * HEAD_WIDTH), D ** -0.5, 0.0625, ((1, 4),))
    store_a = noise(own_keys[4], (N_REPLICA * ASLOT, 2, RANK, D), D ** -0.5, 0.0625, ((0, 4), (3, 4)))
    store_b = noise(own_keys[5], (N_REPLICA * ASLOT, 2, RANK, KEY_VALUE_HEADS * HEAD_WIDTH), RANK ** -0.5, 0.75, ((0, 4), (3, 4)))
    lengths = draw_lengths(jax.random.fold_in(jax.random.fold_in(arg_keys[13], part), 71), part)
    arrival_from = draw_arrival_from(jax.random.fold_in(jax.random.fold_in(arg_keys[13], part), 71), part)
    arrival_slot = draw_arrival_slot(jax.random.fold_in(jax.random.fold_in(arg_keys[13], part), 71), part)
    resident_adapter = with_ends(jax.random.randint(own_keys[9], (N_REPLICA * RES,), 0, ASLOT), jax.random.fold_in(own_keys[9], 1), 0, ASLOT - 1).astype(jnp.int32)
    arrival_adapter = with_ends(jax.random.randint(own_keys[10], (N_REPLICA, ARRIVE), 0, COPIES), jax.random.fold_in(own_keys[10], 1), 0, COPIES - 1).astype(jnp.int32)
    hot_holder = draw_hot_holder(jax.random.fold_in(jax.random.fold_in(arg_keys[13], part), 71), part)
    hot_dest = draw_hot_dest(jax.random.fold_in(jax.random.fold_in(arg_keys[13], part), 71), part)
    return {"hidden": hidden, "queries": queries, "kv_cache": kv_cache, "w_kv": w_kv, "store_a": store_a, "store_b": store_b, "lengths": lengths, "arrival_from": arrival_from, "arrival_slot": arrival_slot, "resident_adapter": resident_adapter, "arrival_adapter": arrival_adapter, "hot_holder": hot_holder, "hot_dest": hot_dest}


ADAPTER_SCALE = 2.0
ROPE_BASE = 500000.0

def rotate_keys(key_rows, positions):
    half_size = HEAD_WIDTH // 2
    frequency = ROPE_BASE ** (-(jnp.arange(half_size, dtype=jnp.float32) * 2.0 / HEAD_WIDTH))
    angles = positions.astype(jnp.float32)[:, :, None, None] * frequency
    cosine = jnp.cos(angles)
    sine_val = jnp.sin(angles)
    first_half = key_rows[..., :half_size]
    second_half = key_rows[..., half_size:]
    return jnp.concatenate([first_half * cosine - second_half * sine_val, second_half * cosine + first_half * sine_val], axis=-1)

def attend(queries, stored, lengths_now, fresh_kv):
    request_slot_count = queries.shape[0]
    group_size = HEADS // KEY_VALUE_HEADS
    grouped = queries.astype(jnp.float32).reshape(request_slot_count, NEW_TOKEN_COUNT, KEY_VALUE_HEADS, group_size, HEAD_WIDTH)
    score_scale = 1.0 / math.sqrt(HEAD_WIDTH)
    past_scores = jnp.einsum('msgjd,mcgd->msgjc', grouped, stored[..., :HEAD_WIDTH].astype(jnp.float32)) * score_scale
    recent_scores = jnp.einsum('msgjd,mtgd->msgjt', grouped, fresh_kv[..., :HEAD_WIDTH].astype(jnp.float32)) * score_scale
    row_ids = jnp.arange(CAP, dtype=jnp.int32)
    past_ok = (row_ids[None, :] < lengths_now[:, None])[:, None, None, None, :]
    step_ids = jnp.arange(NEW_TOKEN_COUNT, dtype=jnp.int32)
    recent_ok = (step_ids[None, :] <= step_ids[:, None])[None, :, None, None, :]
    past_scores = jnp.where(past_ok, past_scores, -jnp.inf)
    recent_scores = jnp.where(recent_ok, recent_scores, -jnp.inf)
    peak_score = jnp.maximum(lax.optimization_barrier(jnp.max(past_scores, -1)), lax.optimization_barrier(jnp.max(recent_scores, -1)))[..., None]
    past_exp = jnp.exp(past_scores - peak_score)
    recent_exp = jnp.exp(recent_scores - peak_score)
    denom_sum = lax.optimization_barrier(jnp.sum(past_exp, -1, keepdims=True)) + lax.optimization_barrier(jnp.sum(recent_exp, -1, keepdims=True))
    past_w = (past_exp / denom_sum).astype(jnp.bfloat16).astype(jnp.float32)
    recent_w = (recent_exp / denom_sum).astype(jnp.bfloat16).astype(jnp.float32)
    mixed_out = jnp.einsum('msgjc,mcgd->msgjd', past_w, stored[..., HEAD_WIDTH:].astype(jnp.float32))
    mixed_out = mixed_out + jnp.einsum('msgjt,mtgd->msgjd', recent_w, fresh_kv[..., HEAD_WIDTH:].astype(jnp.float32))
    return mixed_out.reshape(request_slot_count, NEW_TOKEN_COUNT, HEADS * HEAD_WIDTH)

def reference(hidden, queries, kv_cache, w_kv, store_a, store_b, lengths, arrival_from, arrival_slot, resident_adapter, arrival_adapter, hot_holder, hot_dest):
    request_slot_count = RES + ARRIVE
    leaving_ids = (arrival_from * RES + arrival_slot).reshape(-1)
    blocks = hot_dest.reshape(COPIES, SPANS, FAN)
    weight_f32 = w_kv.astype(jnp.float32)

    def one_replica(replica):
        own_ids = replica * RES + jnp.arange(RES, dtype=jnp.int32)
        moved_ids = arrival_from[replica] * RES + arrival_slot[replica]
        source_ids = jnp.concatenate([own_ids, moved_ids]).astype(jnp.int32)
        staying = jnp.logical_not(jnp.any(own_ids[:, None] == leaving_ids[None, :], axis=1))
        live_mask = jnp.concatenate([staying, jnp.ones((ARRIVE,), bool)])
        seen_len = lengths[source_ids]
        listed = jnp.any(blocks == replica, axis=2).astype(jnp.int32)
        wanted = jnp.arange(COPIES, dtype=jnp.int32) * SPANS + lax.optimization_barrier(jnp.sum(listed * jnp.arange(SPANS, dtype=jnp.int32)[None, :], axis=1))
        inst_a = store_a[hot_holder[wanted]]
        inst_b = store_b[hot_holder[wanted]]
        own_adapter = lax.dynamic_slice_in_dim(resident_adapter, replica * RES, RES)
        my_choice = arrival_adapter[replica]
        adapt_a = jnp.concatenate([store_a[replica * ASLOT + own_adapter], inst_a[my_choice]])
        adapter_up_weight = jnp.concatenate([store_b[replica * ASLOT + own_adapter], inst_b[my_choice]])
        hidden_f32 = lax.dynamic_slice_in_dim(hidden, replica * request_slot_count, request_slot_count).astype(jnp.float32)
        query_rows = lax.dynamic_slice_in_dim(queries, replica * request_slot_count, request_slot_count)
        base_projection = jnp.einsum('msd,dgc->msgc', hidden_f32, weight_f32)
        down_projected = jnp.einsum('msd,mpkd->mspk', hidden_f32, adapt_a.astype(jnp.float32)).astype(jnp.bfloat16)
        adapter_update = jnp.einsum('gnot,gote->gnoe', down_projected.astype(jnp.float32), adapter_up_weight.astype(jnp.float32))
        adapter_update = adapter_update.reshape(request_slot_count, NEW_TOKEN_COUNT, 2, KEY_VALUE_HEADS, HEAD_WIDTH).transpose(0, 1, 3, 2, 4).reshape(request_slot_count, NEW_TOKEN_COUNT, KEY_VALUE_HEADS, 2 * HEAD_WIDTH)
        unrotated_key_value = base_projection + ADAPTER_SCALE * adapter_update
        positions = seen_len[:, None] + jnp.arange(NEW_TOKEN_COUNT, dtype=jnp.int32)[None, :]
        fresh_kv = jnp.concatenate([rotate_keys(unrotated_key_value[..., :HEAD_WIDTH], positions), unrotated_key_value[..., HEAD_WIDTH:]], axis=-1).astype(jnp.bfloat16)
        stored = kv_cache[source_ids]
        row_ids = jnp.arange(CAP, dtype=jnp.int32)
        arrived = jnp.where((row_ids[None, :] < seen_len[RES:, None])[:, :, None, None], stored[RES:], jnp.zeros((), jnp.bfloat16))
        mixed_out = attend(query_rows, stored, seen_len, fresh_kv)
        attn_rows = jnp.where(live_mask[:, None, None], mixed_out, 0.0).astype(jnp.bfloat16)
        fresh_rows = jnp.where(live_mask[:, None, None, None], fresh_kv, jnp.zeros((), jnp.bfloat16))
        return (attn_rows, fresh_rows, arrived, inst_a, inst_b)
    attn_all, fresh_all, arrived_all, inst_a_all, inst_b_all = lax.map(one_replica, jnp.arange(N_REPLICA, dtype=jnp.int32))
    return (attn_all.reshape(N_REPLICA * request_slot_count, NEW_TOKEN_COUNT, HEADS * HEAD_WIDTH), fresh_all.reshape(N_REPLICA * request_slot_count, NEW_TOKEN_COUNT, KEY_VALUE_HEADS, 2 * HEAD_WIDTH), arrived_all.reshape(N_REPLICA * ARRIVE, CAP, KEY_VALUE_HEADS, 2 * HEAD_WIDTH), inst_a_all.reshape(N_REPLICA * COPIES, 2, RANK, D), inst_b_all.reshape(N_REPLICA * COPIES, 2, RANK, KEY_VALUE_HEADS * HEAD_WIDTH))
```

```python
import functools
import math

import jax
import jax.numpy as jnp
from jax import lax
from jax.experimental import pallas as pl
from jax.experimental.pallas import tpu as pltpu
from jax.sharding import PartitionSpec as P

COPIES = 4


ADAPTER_SCALE = 2.0
ROPE_BASE = 500000.0


def rotate_keys(key_rows, positions):
    head_length = key_rows.shape[-1]
    half_size = head_length // 2
    frequency = ROPE_BASE ** (-(jnp.arange(half_size, dtype=jnp.float32) * 2.0 / head_length))
    angles = positions.astype(jnp.float32)[:, :, None, None] * frequency
    cosine = jnp.cos(angles)
    sine_val = jnp.sin(angles)
    first_half = key_rows[..., :half_size]
    second_half = key_rows[..., half_size:]
    return jnp.concatenate(
        [
            first_half * cosine - second_half * sine_val,
            second_half * cosine + first_half * sine_val,
        ],
        axis=-1,
    )


def attend(queries, stored, lengths_now, fresh_kv):
    request_slot_count, decode_step_count, heads_local, head_length = queries.shape
    local_key_value = stored.shape[2]
    group_size = heads_local // local_key_value
    grouped = queries.reshape(
        request_slot_count, decode_step_count, local_key_value, group_size, head_length
    )
    score_scale = 1.0 / math.sqrt(head_length)
    past_scores = (
        jnp.einsum(
            "msgjd,mcgd->msgjc",
            grouped,
            stored[..., :head_length],
            preferred_element_type=jnp.float32,
        )
        * score_scale
    )
    recent_scores = (
        jnp.einsum(
            "msgjd,mtgd->msgjt",
            grouped,
            fresh_kv[..., :head_length],
            preferred_element_type=jnp.float32,
        )
        * score_scale
    )
    row_ids = jnp.arange(stored.shape[1], dtype=jnp.int32)
    past_ok = (row_ids[None, :] < lengths_now[:, None])[:, None, None, None, :]
    step_ids = jnp.arange(decode_step_count, dtype=jnp.int32)
    recent_ok = (step_ids[None, :] <= step_ids[:, None])[None, :, None, None, :]
    past_scores = jnp.where(past_ok, past_scores, -jnp.inf)
    recent_scores = jnp.where(recent_ok, recent_scores, -jnp.inf)
    peak_score = jnp.maximum(jnp.max(past_scores, -1), jnp.max(recent_scores, -1))[..., None]
    past_exp = jnp.exp(past_scores - peak_score)
    recent_exp = jnp.exp(recent_scores - peak_score)
    denom_sum = jnp.sum(past_exp, -1, keepdims=True) + jnp.sum(recent_exp, -1, keepdims=True)
    past_w = (past_exp / denom_sum).astype(jnp.bfloat16)
    recent_w = (recent_exp / denom_sum).astype(jnp.bfloat16)
    mixed_out = jnp.einsum(
        "msgjc,mcgd->msgjd", past_w, stored[..., head_length:], preferred_element_type=jnp.float32
    )
    mixed_out = mixed_out + jnp.einsum(
        "msgjt,mtgd->msgjd",
        recent_w,
        fresh_kv[..., head_length:],
        preferred_element_type=jnp.float32,
    )
    return mixed_out.reshape(request_slot_count, decode_step_count, heads_local * head_length)


def general(
    hidden,
    queries,
    kv_cache,
    w_kv,
    store_a,
    store_b,
    lengths,
    arrival_from,
    arrival_slot,
    resident_adapter,
    arrival_adapter,
    hot_holder,
    hot_dest,
):
    my_index = lax.axis_index("replica")
    replicas = lax.axis_size("replica")
    resident = kv_cache.shape[0]
    arrive = arrival_from.shape[1]
    request_slot_count = resident + arrive
    decode_step_count = hidden.shape[1]
    head_length = queries.shape[3]
    local_key_value = kv_cache.shape[2]
    slot_total = store_a.shape[0]
    hot_total = hot_holder.shape[0]
    spans = hot_total // COPIES
    my_from = lax.dynamic_index_in_dim(arrival_from, my_index, 0, keepdims=False)
    my_slot = lax.dynamic_index_in_dim(arrival_slot, my_index, 0, keepdims=False)
    own_ids = my_index * resident + jnp.arange(resident, dtype=jnp.int32)
    leaving_ids = (arrival_from * resident + arrival_slot).reshape(-1)
    staying = jnp.logical_not(jnp.any(own_ids[:, None] == leaving_ids[None, :], axis=1))
    live_mask = jnp.concatenate([staying, jnp.ones((arrive,), bool)])
    own_len = lax.dynamic_slice_in_dim(lengths, my_index * resident, resident)
    arrival_len = jnp.take(lengths, my_from * resident + my_slot)
    seen_len = jnp.concatenate([own_len, arrival_len])
    takes_mine = arrival_from == my_index
    sends_any = jnp.any(takes_mine, axis=1)
    send_slot = jnp.sum(jnp.where(takes_mine, arrival_slot, 0), axis=1)
    outgoing = jnp.take(kv_cache, send_slot, axis=0)
    outgoing = jnp.where(sends_any[:, None, None, None], outgoing, jnp.zeros((), jnp.bfloat16))
    incoming = lax.all_to_all(outgoing, "replica", split_axis=0, concat_axis=0, tiled=True)
    blocks = hot_dest.reshape(COPIES, spans, hot_dest.shape[1])
    holder_grid = hot_holder.reshape(COPIES, spans)
    holder_rep = holder_grid // slot_total
    mine = holder_rep == my_index
    has_one = jnp.any(mine, axis=1)
    local_pick = jnp.sum(jnp.where(mine, holder_grid % slot_total, 0), axis=1)

    def spread_rows(store):
        rows = jnp.take(store, local_pick, axis=0)
        rows = jnp.where(has_one[:, None, None, None], rows, jnp.zeros((), jnp.bfloat16))
        return rows.reshape(COPIES, replicas, -1).transpose(1, 0, 2)

    got_a, got_b = (
        lax.all_to_all(spread_rows(store_a), "replica", split_axis=0, concat_axis=0, tiled=True),
        lax.all_to_all(spread_rows(store_b), "replica", split_axis=0, concat_axis=0, tiled=True),
    )
    replica_ids = jnp.arange(replicas, dtype=jnp.int32)
    member = jnp.any(blocks[:, :, :, None] == replica_ids[None, None, None, :], axis=2).astype(
        jnp.int32
    )
    source_rep = jnp.sum(member * holder_rep[:, :, None], axis=1)
    copy_ids = jnp.arange(COPIES, dtype=jnp.int32)
    route_a = got_a[source_rep.T, copy_ids[None, :]]
    route_b = got_b[source_rep.T, copy_ids[None, :]]
    recv_a, recv_b = (
        lax.all_to_all(route_a, "replica", split_axis=0, concat_axis=0, tiled=True),
        lax.all_to_all(route_b, "replica", split_axis=0, concat_axis=0, tiled=True),
    )
    installed_a = recv_a.transpose(1, 0, 2).reshape((COPIES,) + store_a.shape[1:])
    installed_b = recv_b.transpose(1, 0, 2).reshape((COPIES,) + store_b.shape[1:])
    own_adapter = lax.dynamic_slice_in_dim(resident_adapter, my_index * resident, resident)
    my_choice = lax.dynamic_index_in_dim(arrival_adapter, my_index, 0, keepdims=False)
    adapt_a = jnp.concatenate(
        [jnp.take(store_a, own_adapter, axis=0), jnp.take(installed_a, my_choice, axis=0)]
    )
    adapter_up_weight = jnp.concatenate(
        [jnp.take(store_b, own_adapter, axis=0), jnp.take(installed_b, my_choice, axis=0)]
    )
    partial_value = jnp.einsum(
        "msd,mpkd->mspk", hidden, adapt_a, preferred_element_type=jnp.float32
    )
    base_projection = jnp.einsum(
        "msd,dgc->msgc",
        lax.all_gather(hidden, "tensor", axis=2, tiled=True),
        w_kv,
        preferred_element_type=jnp.float32,
    )
    down_projected = lax.psum(partial_value, "tensor")
    down_projected = down_projected.astype(jnp.bfloat16)
    adapter_update = jnp.einsum(
        "gnot,gote->gnoe", down_projected, adapter_up_weight, preferred_element_type=jnp.float32
    )
    adapter_update = (
        adapter_update.reshape(
            request_slot_count, decode_step_count, 2, local_key_value, head_length
        )
        .transpose(0, 1, 3, 2, 4)
        .reshape(request_slot_count, decode_step_count, local_key_value, 2 * head_length)
    )
    unrotated_key_value = base_projection + ADAPTER_SCALE * adapter_update
    positions = seen_len[:, None] + jnp.arange(decode_step_count, dtype=jnp.int32)[None, :]
    fresh_kv = jnp.concatenate(
        [
            rotate_keys(unrotated_key_value[..., :head_length], positions),
            unrotated_key_value[..., head_length:],
        ],
        axis=-1,
    ).astype(jnp.bfloat16)
    stay_out = attend(queries[:resident], kv_cache, own_len, fresh_kv[:resident])
    arrived = jnp.take(incoming, my_from, axis=0)
    row_ids = jnp.arange(kv_cache.shape[1], dtype=jnp.int32)
    arrived = jnp.where(
        (row_ids[None, :] < arrival_len[:, None])[:, :, None, None],
        arrived,
        jnp.zeros((), jnp.bfloat16),
    )
    move_out = attend(queries[resident:], arrived, arrival_len, fresh_kv[resident:])
    mixed_out = jnp.concatenate([stay_out, move_out], axis=0)
    attn_out = jnp.where(live_mask[:, None, None], mixed_out, 0.0).astype(jnp.bfloat16)
    new_kv = jnp.where(live_mask[:, None, None, None], fresh_kv, jnp.zeros((), jnp.bfloat16))
    return (attn_out, new_kv, arrived, installed_a, installed_b)


PAIRED = 4


def needed_first(adapter_ref, dest):
    first = adapter_ref[dest, 0]
    second = adapter_ref[dest, 1]
    other = jnp.where(first == 0, 1, 0)
    second = jnp.where(second == first, other, second)
    place, seen = [], jnp.int32(2)
    for c in range(COPIES):
        early = jnp.logical_or(first == c, second == c)
        place.append(jnp.where(first == c, 0, jnp.where(second == c, 1, seen)))
        seen = seen + jnp.where(early, 0, 1)
    order = []
    for j in range(COPIES):
        at = jnp.int32(0)
        for c in range(1, COPIES):
            at = at + jnp.where(place[c] == j, c, 0)
        order.append(at)
    return order, place


def held_slot(holder_ref, spans, slots, replica, copy_id):
    found = jnp.int32(0)
    for s in range(spans):
        holder = holder_ref[copy_id * spans + s]
        found = jnp.where(holder // slots == replica, holder % slots, found)
    return found


def holder_of(holder_ref, dest_ref, spans, dest, copy_id):
    found = jnp.int32(0)
    for s in range(spans):
        row = copy_id * spans + s
        found = jnp.where(dest_ref[row, 0] == dest, holder_ref[row], found)
    return found


def pack_kernel(spans, slots, from_ref, slot_ref, adapter_ref, holder_ref, a_ref, b_ref, kv_ref,
                a0_ref, a1_ref, b_out, k1_ref, k2_ref, k3_ref, sems):
    me = lax.axis_index("replica")
    copies = []

    def go(src, dst):
        copy = pltpu.make_async_copy(src, dst, sems.at[len(copies)])
        copy.start()
        copies.append(copy)

    order, _ = needed_first(adapter_ref, me ^ 3)
    held = [held_slot(holder_ref, spans, slots, me, c) for c in order]
    for j in range(2):
        go(a_ref.at[held[j]], a0_ref.at[j])
    for k, out in ((1, k1_ref), (2, k2_ref), (3, k3_ref)):
        chosen = jnp.int32(0)
        for a in range(2):
            chosen = jnp.where(from_ref[me ^ k, a] == me, slot_ref[me ^ k, a], chosen)
        go(kv_ref.at[chosen], out)
    for j in range(COPIES):
        go(b_ref.at[held[j]], b_out.at[j])
    for j in range(2):
        go(a_ref.at[held[2 + j]], a1_ref.at[j])
    for copy in copies:
        copy.wait()


def pick_kernel(spans, slots, base, count, adapter_ref, holder_ref, dest_ref, store_ref, core_ref, out_ref, sems):
    me = lax.axis_index("replica")
    dest = me ^ 2
    order, _ = needed_first(adapter_ref, dest)
    for j in range(count):
        holder = holder_of(holder_ref, dest_ref, spans, dest, order[base + j])
        mine = holder // slots == me

        @pl.when(mine)
        def _():
            pltpu.make_async_copy(store_ref.at[holder % slots], out_ref.at[j], sems.at[j]).start()

        @pl.when(jnp.logical_not(mine))
        def _():
            pltpu.make_async_copy(core_ref.at[j], out_ref.at[j], sems.at[j]).start()

    for j in range(count):
        pltpu.make_async_copy(core_ref.at[j], out_ref.at[j], sems.at[j]).wait()


def choose(near, place_near, place_far, near_refs, far_refs, dst, sem):
    for wanted, place, refs in ((near, place_near, near_refs), (jnp.logical_not(near), place_far, far_refs)):
        each = COPIES // 2 if len(refs) == 2 else COPIES
        for r, ref in enumerate(refs):
            inside = jnp.logical_and(place >= r * each, place < (r + 1) * each)

            @pl.when(jnp.logical_and(wanted, inside))
            def _():
                pltpu.make_async_copy(ref.at[place - r * each], dst, sem).start()


def arrive_kernel(spans, slots, adapter_ref, holder_ref, dest_ref, hid_ref, c0_ref, c1_ref, x0_ref, cb_ref, xb_ref,
                  out_ref, b_out, units, sems):
    me = lax.axis_index("replica")
    _, place_far = needed_first(adapter_ref, me)
    _, place_near = needed_first(adapter_ref, me ^ 2)

    def at(places, c):
        found = places[0]
        for i in range(1, COPIES):
            found = jnp.where(c == i, places[i], found)
        return found

    for a in range(2):
        c = adapter_ref[me, a]
        near = holder_of(holder_ref, dest_ref, spans, me, c) // slots == (me ^ 1)
        choose(near, at(place_near, c), at(place_far, c), (c0_ref, c1_ref), (x0_ref, x0_ref), units.at[a], sems.at[a])
        choose(near, at(place_near, c), at(place_far, c), (cb_ref,), (xb_ref,), b_out.at[a], sems.at[2 + a])
    for a in range(2):
        pltpu.make_async_copy(c0_ref.at[0], units.at[a], sems.at[a]).wait()
        unit = units[a].reshape(units.shape[1] * units.shape[2], units.shape[3])
        out_ref[a] = lax.dot_general(hid_ref[...], unit, (((1,), (1,)), ((), ())), preferred_element_type=jnp.float32)
        pltpu.make_async_copy(cb_ref.at[0], b_out.at[a], sems.at[2 + a]).wait()


def install_kernel(spans, slots, adapter_ref, holder_ref, dest_ref, c0_ref, c1_ref, x0_ref, x1_ref, cb_ref, xb_ref,
                   a_out, b_out, sems):
    me = lax.axis_index("replica")
    _, place_far = needed_first(adapter_ref, me)
    _, place_near = needed_first(adapter_ref, me ^ 2)
    for c in range(COPIES):
        near = holder_of(holder_ref, dest_ref, spans, me, c) // slots == (me ^ 1)
        choose(near, place_near[c], place_far[c], (c0_ref, c1_ref), (x0_ref, x1_ref), a_out.at[c], sems.at[c])
        choose(near, place_near[c], place_far[c], (cb_ref,), (xb_ref,), b_out.at[c], sems.at[COPIES + c])
    for c in range(COPIES):
        pltpu.make_async_copy(c0_ref.at[0], a_out.at[c], sems.at[c]).wait()
        pltpu.make_async_copy(cb_ref.at[0], b_out.at[c], sems.at[COPIES + c]).wait()


SMEM = pl.BlockSpec(memory_space=pltpu.SMEM)
ANY = pl.BlockSpec(memory_space=pl.ANY)
VMEM = pl.BlockSpec(memory_space=pltpu.VMEM)


def paired(
    hidden,
    queries,
    kv_cache,
    w_kv,
    store_a,
    store_b,
    lengths,
    arrival_from,
    arrival_slot,
    resident_adapter,
    arrival_adapter,
    hot_holder,
    hot_dest,
):
    me = lax.axis_index("replica")
    tensors = lax.axis_size("tensor")
    tensor_index = lax.axis_index("tensor")
    resident, arrive = kv_cache.shape[0], arrival_from.shape[1]
    requests, steps, width = hidden.shape
    head_length, heads = queries.shape[3], kv_cache.shape[2]
    slots = store_a.shape[0]
    spans = hot_holder.shape[0] // COPIES
    kind = store_a.dtype
    unit_a, unit_b, unit_k = store_a.shape[1:], store_b.shape[1:], kv_cache.shape[1:]

    def shaped(*shape, dtype=kind):
        return jax.ShapeDtypeStruct(shape, dtype)

    def swap(array, k):
        return lax.ppermute(array, "replica", [(i, i ^ k) for i in range(PAIRED)])

    def shift(array, k):
        return lax.ppermute(array, "tensor", [(i, (i + k) % tensors) for i in range(tensors)])

    def cost(bytes_accessed, flops=0):
        return pl.CostEstimate(flops=flops, bytes_accessed=bytes_accessed, transcendentals=0)

    size_a, size_b = 2 * math.prod(unit_a), 2 * math.prod(unit_b)

    a0, a1, b_all, k1, k2, k3 = pl.pallas_call(
        functools.partial(pack_kernel, spans, slots),
        out_shape=(shaped(2, *unit_a), shaped(2, *unit_a), shaped(COPIES, *unit_b), shaped(*unit_k), shaped(*unit_k), shaped(*unit_k)),
        in_specs=[SMEM] * 4 + [ANY] * 3,
        out_specs=(ANY,) * 6,
        scratch_shapes=[pltpu.SemaphoreType.DMA((4 + COPIES + 3,))],
        cost_estimate=cost(8 * size_a + 8 * size_b),
    )(arrival_from, arrival_slot, arrival_adapter, hot_holder, store_a, store_b, kv_cache)
    core_a0, core_b = swap(a0, 1), swap(b_all, 1)
    core_a1 = swap(a1, 1)
    far = (swap(k2, 2), swap(k3, 3))
    near = swap(k1, 1)
    pieces = [hidden] + [shift(hidden, k) for k in range(1, tensors)]

    def pick(base, count, store, core):
        return pl.pallas_call(
            functools.partial(pick_kernel, spans, slots, base, count),
            out_shape=shaped(count, *store.shape[1:]),
            in_specs=[SMEM] * 3 + [ANY] * 2,
            out_specs=ANY,
            scratch_shapes=[pltpu.SemaphoreType.DMA((count,))],
            cost_estimate=cost(4 * count * math.prod(store.shape[1:])),
        )(arrival_adapter, hot_holder, hot_dest, store, core)

    far_b = swap(pick(0, COPIES, store_b, core_b), 2)
    far_a0 = swap(pick(0, 2, store_a, core_a0), 2)
    far_a1 = swap(pick(2, 2, store_a, core_a1), 2)

    own_adapter = lax.dynamic_slice_in_dim(resident_adapter, me * resident, resident)
    every = jnp.einsum("msd,epkd->msepk", hidden[:resident], store_a, preferred_element_type=jnp.float32)
    is_own = own_adapter[:, None] == jnp.arange(slots, dtype=jnp.int32)[None, :]
    part_own = jnp.sum(jnp.where(is_own[:, None, :, None, None], every, 0.0), axis=2)

    def total(part):
        out = part
        for k in range(1, tensors):
            out = out + shift(part, k)
        return out.astype(jnp.bfloat16)

    shrink_own = total(part_own.reshape(resident * steps, -1)).reshape(resident, steps, 2, -1)
    whole = jnp.concatenate(pieces, axis=2)
    whole = whole.reshape(requests, steps, tensors, width)
    turn = (tensor_index - jnp.arange(tensors, dtype=jnp.int32)) % tensors
    whole = jnp.take(whole, turn, axis=2).reshape(requests, steps, tensors * width)
    base = jnp.einsum("msd,dgc->msgc", whole, w_kv, preferred_element_type=jnp.float32)

    my_from = lax.dynamic_index_in_dim(arrival_from, me, 0, keepdims=False)
    my_slot = lax.dynamic_index_in_dim(arrival_slot, me, 0, keepdims=False)
    own_ids = me * resident + jnp.arange(resident, dtype=jnp.int32)
    leaving = (arrival_from * resident + arrival_slot).reshape(-1)
    staying = jnp.logical_not(jnp.any(own_ids[:, None] == leaving[None, :], axis=1))
    own_len = lax.dynamic_slice_in_dim(lengths, me * resident, resident)
    arrival_len = jnp.take(lengths, my_from * resident + my_slot)

    def fresh_rows(base_rows, shrink, up, seen):
        count = base_rows.shape[0]
        update = jnp.einsum("gnot,gote->gnoe", shrink, up, preferred_element_type=jnp.float32)
        update = update.reshape(count, steps, 2, heads, head_length).transpose(0, 1, 3, 2, 4)
        raw = base_rows + ADAPTER_SCALE * update.reshape(count, steps, heads, 2 * head_length)
        positions = seen[:, None] + jnp.arange(steps, dtype=jnp.int32)[None, :]
        turned = rotate_keys(raw[..., :head_length], positions)
        return jnp.concatenate([turned, raw[..., head_length:]], axis=-1).astype(jnp.bfloat16)

    up_own = jnp.take(store_b, own_adapter, axis=0)
    fresh_own = fresh_rows(base[:resident], shrink_own, up_own, own_len)
    stay_out = attend(queries[:resident], kv_cache, own_len, fresh_own)
    stay_out = jnp.where(staying[:, None, None], stay_out, 0.0).astype(jnp.bfloat16)
    stay_kv = jnp.where(staying[:, None, None, None], fresh_own, jnp.zeros((), jnp.bfloat16))

    way = (my_from ^ me)[:, None, None, None]
    arrived = jnp.where(way == 1, near[None], jnp.where(way == 2, far[0][None], far[1][None]))
    row_ids = jnp.arange(kv_cache.shape[1], dtype=jnp.int32)
    arrived = jnp.where((row_ids[None, :] < arrival_len[:, None])[:, :, None, None], arrived, jnp.zeros((), jnp.bfloat16))
    rows = 16
    guests = jnp.pad(hidden[resident:].reshape(arrive * steps, width), ((0, rows - arrive * steps), (0, 0)))
    part_new, up_new = pl.pallas_call(
        functools.partial(arrive_kernel, spans, slots),
        out_shape=(shaped(arrive, rows, math.prod(unit_a[:2]), dtype=jnp.float32), shaped(arrive, *unit_b)),
        in_specs=[SMEM] * 3 + [VMEM] + [ANY] * 5,
        out_specs=(VMEM, ANY),
        scratch_shapes=[pltpu.VMEM((arrive,) + unit_a, kind), pltpu.SemaphoreType.DMA((2 * arrive,))],
        cost_estimate=cost(arrive * (size_a + 2 * size_b), 2 * arrive * rows * size_a // 2),
    )(arrival_adapter, hot_holder, hot_dest, guests, core_a0, core_a1, far_a0, core_b, far_b)
    part_new = jnp.concatenate([part_new[a, a * steps : (a + 1) * steps] for a in range(arrive)], axis=0)
    shrink_new = total(part_new).reshape(arrive, steps, 2, -1)
    fresh_new = fresh_rows(base[resident:], shrink_new, up_new, arrival_len)
    move_out = attend(queries[resident:], arrived, arrival_len, fresh_new).astype(jnp.bfloat16)

    attn_out = jnp.concatenate([stay_out, move_out], axis=0)
    new_kv = jnp.concatenate([stay_kv, fresh_new], axis=0)
    installed_a, installed_b = pl.pallas_call(
        functools.partial(install_kernel, spans, slots),
        out_shape=(shaped(COPIES, *unit_a), shaped(COPIES, *unit_b)),
        in_specs=[SMEM] * 3 + [ANY] * 6,
        out_specs=(ANY, ANY),
        scratch_shapes=[pltpu.SemaphoreType.DMA((2 * COPIES,))],
        cost_estimate=cost(8 * size_a + 8 * size_b),
    )(arrival_adapter, hot_holder, hot_dest, core_a0, core_a1, far_a0, far_a1, core_b, far_b)
    return (attn_out, new_kv, arrived, installed_a, installed_b)


def solution(mesh):
    in_specs = (
        P(("parts", "replica"), None, "tensor"),
        P(("parts", "replica"), None, "tensor", None),
        P(("parts", "replica"), None, "tensor", None),
        P(None, "tensor", None),
        P(("parts", "replica"), None, None, "tensor"),
        P(("parts", "replica"), None, None, "tensor"),
        P("parts"),
        P("parts", None),
        P("parts", None),
        P("parts"),
        P("parts", None),
        P("parts"),
        P("parts", None),
    )
    out_specs = (
        P(("parts", "replica"), None, "tensor"),
        P(("parts", "replica"), None, "tensor", None),
        P(("parts", "replica"), None, "tensor", None),
        P(("parts", "replica"), None, None, "tensor"),
        P(("parts", "replica"), None, None, "tensor"),
    )
    local = paired if mesh.shape["replica"] == PAIRED else general
    return jax.shard_map(local, mesh=mesh, in_specs=in_specs, out_specs=out_specs, check_vma=False)
```

```python
import functools
import math

import jax
import jax.numpy as jnp
from jax import lax
from jax.experimental import pallas as pl
from jax.experimental.pallas import tpu as pltpu
from jax.sharding import PartitionSpec as P

COPIES = 4


ADAPTER_SCALE = 2.0
ROPE_BASE = 500000.0


def rotate_keys(key_rows, positions):
    head_length = key_rows.shape[-1]
    half_size = head_length // 2
    frequency = ROPE_BASE ** (-(jnp.arange(half_size, dtype=jnp.float32) * 2.0 / head_length))
    angles = positions.astype(jnp.float32)[:, :, None, None] * frequency
    cosine = jnp.cos(angles)
    sine_val = jnp.sin(angles)
    first_half = key_rows[..., :half_size]
    second_half = key_rows[..., half_size:]
    return jnp.concatenate(
        [
            first_half * cosine - second_half * sine_val,
            second_half * cosine + first_half * sine_val,
        ],
        axis=-1,
    )


def attend(queries, stored, lengths_now, fresh_kv):
    request_slot_count, decode_step_count, heads_local, head_length = queries.shape
    local_key_value = stored.shape[2]
    group_size = heads_local // local_key_value
    grouped = queries.reshape(
        request_slot_count, decode_step_count, local_key_value, group_size, head_length
    )
    score_scale = 1.0 / math.sqrt(head_length)
    past_scores = (
        jnp.einsum(
            "msgjd,mcgd->msgjc",
            grouped,
            stored[..., :head_length],
            preferred_element_type=jnp.float32,
        )
        * score_scale
    )
    recent_scores = (
        jnp.einsum(
            "msgjd,mtgd->msgjt",
            grouped,
            fresh_kv[..., :head_length],
            preferred_element_type=jnp.float32,
        )
        * score_scale
    )
    row_ids = jnp.arange(stored.shape[1], dtype=jnp.int32)
    past_ok = (row_ids[None, :] < lengths_now[:, None])[:, None, None, None, :]
    step_ids = jnp.arange(decode_step_count, dtype=jnp.int32)
    recent_ok = (step_ids[None, :] <= step_ids[:, None])[None, :, None, None, :]
    past_scores = jnp.where(past_ok, past_scores, -jnp.inf)
    recent_scores = jnp.where(recent_ok, recent_scores, -jnp.inf)
    peak_score = jnp.maximum(jnp.max(past_scores, -1), jnp.max(recent_scores, -1))[..., None]
    past_exp = jnp.exp(past_scores - peak_score)
    recent_exp = jnp.exp(recent_scores - peak_score)
    denom_sum = jnp.sum(past_exp, -1, keepdims=True) + jnp.sum(recent_exp, -1, keepdims=True)
    past_w = (past_exp / denom_sum).astype(jnp.bfloat16)
    recent_w = (recent_exp / denom_sum).astype(jnp.bfloat16)
    mixed_out = jnp.einsum(
        "msgjc,mcgd->msgjd", past_w, stored[..., head_length:], preferred_element_type=jnp.float32
    )
    mixed_out = mixed_out + jnp.einsum(
        "msgjt,mtgd->msgjd",
        recent_w,
        fresh_kv[..., head_length:],
        preferred_element_type=jnp.float32,
    )
    return mixed_out.reshape(request_slot_count, decode_step_count, heads_local * head_length)


def general(
    hidden,
    queries,
    kv_cache,
    w_kv,
    store_a,
    store_b,
    lengths,
    arrival_from,
    arrival_slot,
    resident_adapter,
    arrival_adapter,
    hot_holder,
    hot_dest,
):
    my_index = lax.axis_index("replica")
    replicas = lax.axis_size("replica")
    resident = kv_cache.shape[0]
    arrive = arrival_from.shape[1]
    request_slot_count = resident + arrive
    decode_step_count = hidden.shape[1]
    head_length = queries.shape[3]
    local_key_value = kv_cache.shape[2]
    slot_total = store_a.shape[0]
    hot_total = hot_holder.shape[0]
    spans = hot_total // COPIES
    my_from = lax.dynamic_index_in_dim(arrival_from, my_index, 0, keepdims=False)
    my_slot = lax.dynamic_index_in_dim(arrival_slot, my_index, 0, keepdims=False)
    own_ids = my_index * resident + jnp.arange(resident, dtype=jnp.int32)
    leaving_ids = (arrival_from * resident + arrival_slot).reshape(-1)
    staying = jnp.logical_not(jnp.any(own_ids[:, None] == leaving_ids[None, :], axis=1))
    live_mask = jnp.concatenate([staying, jnp.ones((arrive,), bool)])
    own_len = lax.dynamic_slice_in_dim(lengths, my_index * resident, resident)
    arrival_len = jnp.take(lengths, my_from * resident + my_slot)
    seen_len = jnp.concatenate([own_len, arrival_len])
    takes_mine = arrival_from == my_index
    sends_any = jnp.any(takes_mine, axis=1)
    send_slot = jnp.sum(jnp.where(takes_mine, arrival_slot, 0), axis=1)
    outgoing = jnp.take(kv_cache, send_slot, axis=0)
    outgoing = jnp.where(sends_any[:, None, None, None], outgoing, jnp.zeros((), jnp.bfloat16))
    incoming = lax.all_to_all(outgoing, "replica", split_axis=0, concat_axis=0, tiled=True)
    blocks = hot_dest.reshape(COPIES, spans, hot_dest.shape[1])
    holder_grid = hot_holder.reshape(COPIES, spans)
    holder_rep = holder_grid // slot_total
    mine = holder_rep == my_index
    has_one = jnp.any(mine, axis=1)
    local_pick = jnp.sum(jnp.where(mine, holder_grid % slot_total, 0), axis=1)

    def spread_rows(store):
        rows = jnp.take(store, local_pick, axis=0)
        rows = jnp.where(has_one[:, None, None, None], rows, jnp.zeros((), jnp.bfloat16))
        return rows.reshape(COPIES, replicas, -1).transpose(1, 0, 2)

    got_a, got_b = (
        lax.all_to_all(spread_rows(store_a), "replica", split_axis=0, concat_axis=0, tiled=True),
        lax.all_to_all(spread_rows(store_b), "replica", split_axis=0, concat_axis=0, tiled=True),
    )
    replica_ids = jnp.arange(replicas, dtype=jnp.int32)
    member = jnp.any(blocks[:, :, :, None] == replica_ids[None, None, None, :], axis=2).astype(
        jnp.int32
    )
    source_rep = jnp.sum(member * holder_rep[:, :, None], axis=1)
    copy_ids = jnp.arange(COPIES, dtype=jnp.int32)
    route_a = got_a[source_rep.T, copy_ids[None, :]]
    route_b = got_b[source_rep.T, copy_ids[None, :]]
    recv_a, recv_b = (
        lax.all_to_all(route_a, "replica", split_axis=0, concat_axis=0, tiled=True),
        lax.all_to_all(route_b, "replica", split_axis=0, concat_axis=0, tiled=True),
    )
    installed_a = recv_a.transpose(1, 0, 2).reshape((COPIES,) + store_a.shape[1:])
    installed_b = recv_b.transpose(1, 0, 2).reshape((COPIES,) + store_b.shape[1:])
    own_adapter = lax.dynamic_slice_in_dim(resident_adapter, my_index * resident, resident)
    my_choice = lax.dynamic_index_in_dim(arrival_adapter, my_index, 0, keepdims=False)
    adapt_a = jnp.concatenate(
        [jnp.take(store_a, own_adapter, axis=0), jnp.take(installed_a, my_choice, axis=0)]
    )
    adapter_up_weight = jnp.concatenate(
        [jnp.take(store_b, own_adapter, axis=0), jnp.take(installed_b, my_choice, axis=0)]
    )
    partial_value = jnp.einsum(
        "msd,mpkd->mspk", hidden, adapt_a, preferred_element_type=jnp.float32
    )
    base_projection = jnp.einsum(
        "msd,dgc->msgc",
        lax.all_gather(hidden, "tensor", axis=2, tiled=True),
        w_kv,
        preferred_element_type=jnp.float32,
    )
    down_projected = lax.psum(partial_value, "tensor")
    down_projected = down_projected.astype(jnp.bfloat16)
    adapter_update = jnp.einsum(
        "gnot,gote->gnoe", down_projected, adapter_up_weight, preferred_element_type=jnp.float32
    )
    adapter_update = (
        adapter_update.reshape(
            request_slot_count, decode_step_count, 2, local_key_value, head_length
        )
        .transpose(0, 1, 3, 2, 4)
        .reshape(request_slot_count, decode_step_count, local_key_value, 2 * head_length)
    )
    unrotated_key_value = base_projection + ADAPTER_SCALE * adapter_update
    positions = seen_len[:, None] + jnp.arange(decode_step_count, dtype=jnp.int32)[None, :]
    fresh_kv = jnp.concatenate(
        [
            rotate_keys(unrotated_key_value[..., :head_length], positions),
            unrotated_key_value[..., head_length:],
        ],
        axis=-1,
    ).astype(jnp.bfloat16)
    stay_out = attend(queries[:resident], kv_cache, own_len, fresh_kv[:resident])
    arrived = jnp.take(incoming, my_from, axis=0)
    row_ids = jnp.arange(kv_cache.shape[1], dtype=jnp.int32)
    arrived = jnp.where(
        (row_ids[None, :] < arrival_len[:, None])[:, :, None, None],
        arrived,
        jnp.zeros((), jnp.bfloat16),
    )
    move_out = attend(queries[resident:], arrived, arrival_len, fresh_kv[resident:])
    mixed_out = jnp.concatenate([stay_out, move_out], axis=0)
    attn_out = jnp.where(live_mask[:, None, None], mixed_out, 0.0).astype(jnp.bfloat16)
    new_kv = jnp.where(live_mask[:, None, None, None], fresh_kv, jnp.zeros((), jnp.bfloat16))
    return (attn_out, new_kv, arrived, installed_a, installed_b)


PAIRED = 4


def needed_first(adapter_ref, dest):
    first = adapter_ref[dest, 0]
    second = adapter_ref[dest, 1]
    other = jnp.where(first == 0, 1, 0)
    second = jnp.where(second == first, other, second)
    place, seen = [], jnp.int32(2)
    for c in range(COPIES):
        early = jnp.logical_or(first == c, second == c)
        place.append(jnp.where(first == c, 0, jnp.where(second == c, 1, seen)))
        seen = seen + jnp.where(early, 0, 1)
    order = []
    for j in range(COPIES):
        at = jnp.int32(0)
        for c in range(1, COPIES):
            at = at + jnp.where(place[c] == j, c, 0)
        order.append(at)
    return order, place


def held_slot(holder_ref, spans, slots, replica, copy_id):
    found = jnp.int32(0)
    for s in range(spans):
        holder = holder_ref[copy_id * spans + s]
        found = jnp.where(holder // slots == replica, holder % slots, found)
    return found


def holder_of(holder_ref, dest_ref, spans, dest, copy_id):
    found = jnp.int32(0)
    for s in range(spans):
        row = copy_id * spans + s
        found = jnp.where(dest_ref[row, 0] == dest, holder_ref[row], found)
    return found


class Staged:
    def __init__(self, sems):
        self.sems, self.jobs = sems, []

    def go(self, src, stage, dst):
        pltpu.make_async_copy(src, stage, self.sems.at[len(self.jobs)]).start()
        self.jobs.append((stage, dst))

    def finish(self):
        half = len(self.jobs)
        for i, (stage, dst) in enumerate(self.jobs):
            pltpu.make_async_copy(dst, stage, self.sems.at[i]).wait()
            pltpu.make_async_copy(stage, dst, self.sems.at[half + i]).start()
        for i, (stage, dst) in enumerate(self.jobs):
            pltpu.make_async_copy(stage, dst, self.sems.at[half + i]).wait()


def pack_kernel(spans, slots, from_hbm, slot_hbm, adapter_hbm, holder_hbm, a_ref, b_ref, kv_ref,
                a0_ref, a1_ref, b_out, k1_ref, k2_ref, k3_ref,
                from_ref, slot_ref, adapter_ref, holder_ref, a_stage, b_stage, k_stage, small_sems, sems):
    me = lax.axis_index("replica")
    small = [
        pltpu.make_async_copy(src, dst, small_sems.at[i])
        for i, (src, dst) in enumerate(
            ((adapter_hbm, adapter_ref), (holder_hbm, holder_ref), (from_hbm, from_ref), (slot_hbm, slot_ref))
        )
    ]
    for copy in small:
        copy.start()
    for copy in small:
        copy.wait()
    staged = Staged(sems)

    order, _ = needed_first(adapter_ref, me ^ 3)
    held = [held_slot(holder_ref, spans, slots, me, c) for c in order]
    for j in range(2):
        staged.go(a_ref.at[held[j]], a_stage.at[j], a0_ref.at[j])
    for j in range(COPIES):
        staged.go(b_ref.at[held[j]], b_stage.at[j], b_out.at[j])
    for k, out in ((1, k1_ref), (2, k2_ref), (3, k3_ref)):
        chosen = jnp.int32(0)
        for a in range(2):
            chosen = jnp.where(from_ref[me ^ k, a] == me, slot_ref[me ^ k, a], chosen)
        staged.go(kv_ref.at[chosen], k_stage.at[k - 1], out)
    for j in range(2):
        staged.go(a_ref.at[held[2 + j]], a_stage.at[2 + j], a1_ref.at[j])
    staged.finish()


def pick_kernel(spans, slots, base, count, adapter_ref, holder_ref, dest_ref, store_ref, core_ref, out_ref, stage, sems):
    me = lax.axis_index("replica")
    dest = me ^ 2
    order, _ = needed_first(adapter_ref, dest)
    for j in range(count):
        holder = holder_of(holder_ref, dest_ref, spans, dest, order[base + j])
        mine = holder // slots == me

        @pl.when(mine)
        def _():
            pltpu.make_async_copy(store_ref.at[holder % slots], stage.at[j], sems.at[j]).start()

        @pl.when(jnp.logical_not(mine))
        def _():
            pltpu.make_async_copy(core_ref.at[j], stage.at[j], sems.at[j]).start()

    for j in range(count):
        pltpu.make_async_copy(core_ref.at[j], stage.at[j], sems.at[j]).wait()
        pltpu.make_async_copy(stage.at[j], out_ref.at[j], sems.at[count + j]).start()
    for j in range(count):
        pltpu.make_async_copy(stage.at[j], out_ref.at[j], sems.at[count + j]).wait()


def choose(near, place_near, place_far, near_refs, far_refs, dst, sem):
    for wanted, place, refs in ((near, place_near, near_refs), (jnp.logical_not(near), place_far, far_refs)):
        each = COPIES // 2 if len(refs) == 2 else COPIES
        for r, ref in enumerate(refs):
            inside = jnp.logical_and(place >= r * each, place < (r + 1) * each)

            @pl.when(jnp.logical_and(wanted, inside))
            def _():
                pltpu.make_async_copy(ref.at[place - r * each], dst, sem).start()


def arrive_kernel(spans, slots, adapter_ref, holder_ref, dest_ref, hid_ref, c0_ref, c1_ref, x0_ref, cb_ref, xb_ref,
                  out_ref, b_out, units, sems):
    me = lax.axis_index("replica")
    _, place_far = needed_first(adapter_ref, me)
    _, place_near = needed_first(adapter_ref, me ^ 2)

    def at(places, c):
        found = places[0]
        for i in range(1, COPIES):
            found = jnp.where(c == i, places[i], found)
        return found

    for a in range(2):
        c = adapter_ref[me, a]
        near = holder_of(holder_ref, dest_ref, spans, me, c) // slots == (me ^ 1)
        choose(near, at(place_near, c), at(place_far, c), (c0_ref, c1_ref), (x0_ref, x0_ref), units.at[a], sems.at[a])
        choose(near, at(place_near, c), at(place_far, c), (cb_ref,), (xb_ref,), b_out.at[a], sems.at[2 + a])
    for a in range(2):
        pltpu.make_async_copy(c0_ref.at[0], units.at[a], sems.at[a]).wait()
        unit = units[a].reshape(units.shape[1] * units.shape[2], units.shape[3])
        out_ref[a] = lax.dot_general(hid_ref[...], unit, (((1,), (1,)), ((), ())), preferred_element_type=jnp.float32)
        pltpu.make_async_copy(cb_ref.at[0], b_out.at[a], sems.at[2 + a]).wait()


def install_kernel(spans, slots, adapter_ref, holder_ref, dest_ref, c0_ref, c1_ref, x0_ref, x1_ref, cb_ref, xb_ref,
                   a_out, b_out, a_stage, b_stage, sems):
    me = lax.axis_index("replica")
    _, place_far = needed_first(adapter_ref, me)
    _, place_near = needed_first(adapter_ref, me ^ 2)
    for c in range(COPIES):
        near = holder_of(holder_ref, dest_ref, spans, me, c) // slots == (me ^ 1)
        choose(near, place_near[c], place_far[c], (c0_ref, c1_ref), (x0_ref, x1_ref), a_stage.at[c], sems.at[c])
        choose(near, place_near[c], place_far[c], (cb_ref,), (xb_ref,), b_stage.at[c], sems.at[COPIES + c])
    for c in range(COPIES):
        pltpu.make_async_copy(c0_ref.at[0], a_stage.at[c], sems.at[c]).wait()
        pltpu.make_async_copy(a_stage.at[c], a_out.at[c], sems.at[2 * COPIES + c]).start()
        pltpu.make_async_copy(cb_ref.at[0], b_stage.at[c], sems.at[COPIES + c]).wait()
        pltpu.make_async_copy(b_stage.at[c], b_out.at[c], sems.at[3 * COPIES + c]).start()
    for c in range(COPIES):
        pltpu.make_async_copy(a_stage.at[c], a_out.at[c], sems.at[2 * COPIES + c]).wait()
        pltpu.make_async_copy(b_stage.at[c], b_out.at[c], sems.at[3 * COPIES + c]).wait()


SMEM = pl.BlockSpec(memory_space=pltpu.SMEM)
ANY = pl.BlockSpec(memory_space=pl.ANY)
VMEM = pl.BlockSpec(memory_space=pltpu.VMEM)


def paired(
    hidden,
    queries,
    kv_cache,
    w_kv,
    store_a,
    store_b,
    lengths,
    arrival_from,
    arrival_slot,
    resident_adapter,
    arrival_adapter,
    hot_holder,
    hot_dest,
):
    me = lax.axis_index("replica")
    tensors = lax.axis_size("tensor")
    tensor_index = lax.axis_index("tensor")
    resident, arrive = kv_cache.shape[0], arrival_from.shape[1]
    requests, steps, width = hidden.shape
    head_length, heads = queries.shape[3], kv_cache.shape[2]
    slots = store_a.shape[0]
    spans = hot_holder.shape[0] // COPIES
    kind = store_a.dtype
    unit_a, unit_b, unit_k = store_a.shape[1:], store_b.shape[1:], kv_cache.shape[1:]

    def shaped(*shape, dtype=kind):
        return jax.ShapeDtypeStruct(shape, dtype)

    def swap(array, k):
        return lax.ppermute(array, "replica", [(i, i ^ k) for i in range(PAIRED)])

    def shift(array, k):
        return lax.ppermute(array, "tensor", [(i, (i + k) % tensors) for i in range(tensors)])

    def cost(bytes_accessed, flops=0):
        return pl.CostEstimate(flops=flops, bytes_accessed=bytes_accessed, transcendentals=0)

    size_a, size_b = 2 * math.prod(unit_a), 2 * math.prod(unit_b)

    a0, a1, b_all, k1, k2, k3 = pl.pallas_call(
        functools.partial(pack_kernel, spans, slots),
        out_shape=(shaped(2, *unit_a), shaped(2, *unit_a), shaped(COPIES, *unit_b), shaped(*unit_k), shaped(*unit_k), shaped(*unit_k)),
        in_specs=[ANY] * 7,
        out_specs=(ANY,) * 6,
        scratch_shapes=[pltpu.SMEM(x.shape, x.dtype) for x in (arrival_from, arrival_slot, arrival_adapter, hot_holder)]
        + [
            pltpu.VMEM((COPIES,) + unit_a, kind),
            pltpu.VMEM((COPIES,) + unit_b, kind),
            pltpu.VMEM((3,) + unit_k, kind),
            pltpu.SemaphoreType.DMA((4,)),
            pltpu.SemaphoreType.DMA((2 * (2 * COPIES + 3),)),
        ],
        cost_estimate=cost(8 * size_a + 8 * size_b),
    )(arrival_from, arrival_slot, arrival_adapter, hot_holder, store_a, store_b, kv_cache)
    core_a0, core_b = swap(a0, 1), swap(b_all, 1)
    core_a1 = swap(a1, 1)
    far = (swap(k2, 2), swap(k3, 3))
    near = swap(k1, 1)
    a0, hidden = lax.optimization_barrier((a0, hidden))

    def pick(base, count, store, core):
        return pl.pallas_call(
            functools.partial(pick_kernel, spans, slots, base, count),
            out_shape=shaped(count, *store.shape[1:]),
            in_specs=[SMEM] * 3 + [ANY] * 2,
            out_specs=ANY,
            scratch_shapes=[pltpu.VMEM((count,) + store.shape[1:], kind), pltpu.SemaphoreType.DMA((2 * count,))],
            cost_estimate=cost(4 * count * math.prod(store.shape[1:])),
        )(arrival_adapter, hot_holder, hot_dest, store, core)

    to_a0 = pick(0, 2, store_a, core_a0)
    far_a0 = swap(to_a0, 2)
    to_b = pick(0, COPIES, store_b, core_b)
    far_b = swap(to_b, 2)
    to_a1 = pick(2, 2, store_a, core_a1)
    far_a1 = swap(to_a1, 2)

    own_adapter = lax.dynamic_slice_in_dim(resident_adapter, me * resident, resident)
    every = jnp.einsum("msd,epkd->msepk", hidden[:resident], store_a, preferred_element_type=jnp.float32)
    is_own = own_adapter[:, None] == jnp.arange(slots, dtype=jnp.int32)[None, :]
    part_own = jnp.sum(jnp.where(is_own[:, None, :, None, None], every, 0.0), axis=2)

    _, hidden, part_own, queries, lengths, own_adapter, kv_cache = lax.optimization_barrier(
        (to_a1, hidden, part_own, queries, lengths, own_adapter, kv_cache)
    )
    pieces = [hidden] + [shift(hidden, k) for k in range(1, tensors)]

    def total(part):
        out = part
        for k in range(1, tensors):
            out = out + shift(part, k)
        return out.astype(jnp.bfloat16)

    shrink_own = total(part_own.reshape(resident * steps, -1)).reshape(resident, steps, 2, -1)
    whole = jnp.concatenate(pieces, axis=2)
    whole = whole.reshape(requests, steps, tensors, width)
    turn = (tensor_index - jnp.arange(tensors, dtype=jnp.int32)) % tensors
    whole = jnp.take(whole, turn, axis=2).reshape(requests, steps, tensors * width)
    base = jnp.einsum("msd,dgc->msgc", whole, w_kv, preferred_element_type=jnp.float32)

    my_from = lax.dynamic_index_in_dim(arrival_from, me, 0, keepdims=False)
    my_slot = lax.dynamic_index_in_dim(arrival_slot, me, 0, keepdims=False)
    own_ids = me * resident + jnp.arange(resident, dtype=jnp.int32)
    leaving = (arrival_from * resident + arrival_slot).reshape(-1)
    staying = jnp.logical_not(jnp.any(own_ids[:, None] == leaving[None, :], axis=1))
    own_len = lax.dynamic_slice_in_dim(lengths, me * resident, resident)
    arrival_len = jnp.take(lengths, my_from * resident + my_slot)

    def fresh_rows(base_rows, shrink, up, seen):
        count = base_rows.shape[0]
        update = jnp.einsum("gnot,gote->gnoe", shrink, up, preferred_element_type=jnp.float32)
        update = update.reshape(count, steps, 2, heads, head_length).transpose(0, 1, 3, 2, 4)
        raw = base_rows + ADAPTER_SCALE * update.reshape(count, steps, heads, 2 * head_length)
        positions = seen[:, None] + jnp.arange(steps, dtype=jnp.int32)[None, :]
        turned = rotate_keys(raw[..., :head_length], positions)
        return jnp.concatenate([turned, raw[..., head_length:]], axis=-1).astype(jnp.bfloat16)

    up_own = jnp.take(store_b, own_adapter, axis=0)
    fresh_own = fresh_rows(base[:resident], shrink_own, up_own, own_len)
    stay_out = attend(queries[:resident], kv_cache, own_len, fresh_own)
    stay_out = jnp.where(staying[:, None, None], stay_out, 0.0).astype(jnp.bfloat16)
    stay_kv = jnp.where(staying[:, None, None, None], fresh_own, jnp.zeros((), jnp.bfloat16))

    way = (my_from ^ me)[:, None, None, None]
    arrived = jnp.where(way == 1, near[None], jnp.where(way == 2, far[0][None], far[1][None]))
    row_ids = jnp.arange(kv_cache.shape[1], dtype=jnp.int32)
    arrived = jnp.where((row_ids[None, :] < arrival_len[:, None])[:, :, None, None], arrived, jnp.zeros((), jnp.bfloat16))
    rows = 16
    guests = jnp.pad(hidden[resident:].reshape(arrive * steps, width), ((0, rows - arrive * steps), (0, 0)))
    part_new, up_new = pl.pallas_call(
        functools.partial(arrive_kernel, spans, slots),
        out_shape=(shaped(arrive, rows, math.prod(unit_a[:2]), dtype=jnp.float32), shaped(arrive, *unit_b)),
        in_specs=[SMEM] * 3 + [VMEM] + [ANY] * 5,
        out_specs=(VMEM, VMEM),
        scratch_shapes=[pltpu.VMEM((arrive,) + unit_a, kind), pltpu.SemaphoreType.DMA((2 * arrive,))],
        cost_estimate=cost(arrive * (size_a + 2 * size_b), 2 * arrive * rows * size_a // 2),
    )(arrival_adapter, hot_holder, hot_dest, guests, core_a0, core_a1, far_a0, core_b, far_b)
    part_new = jnp.concatenate([part_new[a, a * steps : (a + 1) * steps] for a in range(arrive)], axis=0)
    shrink_new = total(part_new).reshape(arrive, steps, 2, -1)
    fresh_new = fresh_rows(base[resident:], shrink_new, up_new, arrival_len)
    move_out = attend(queries[resident:], arrived, arrival_len, fresh_new).astype(jnp.bfloat16)

    attn_out = jnp.concatenate([stay_out, move_out], axis=0)
    new_kv = jnp.concatenate([stay_kv, fresh_new], axis=0)
    installed_a, installed_b = pl.pallas_call(
        functools.partial(install_kernel, spans, slots),
        out_shape=(shaped(COPIES, *unit_a), shaped(COPIES, *unit_b)),
        in_specs=[SMEM] * 3 + [ANY] * 6,
        out_specs=(ANY, ANY),
        scratch_shapes=[
            pltpu.VMEM((COPIES,) + unit_a, kind),
            pltpu.VMEM((COPIES,) + unit_b, kind),
            pltpu.SemaphoreType.DMA((4 * COPIES,)),
        ],
        cost_estimate=cost(8 * size_a + 8 * size_b),
    )(arrival_adapter, hot_holder, hot_dest, core_a0, core_a1, far_a0, far_a1, core_b, far_b)
    return (attn_out, new_kv, arrived, installed_a, installed_b)


def solution(mesh):
    in_specs = (
        P(("parts", "replica"), None, "tensor"),
        P(("parts", "replica"), None, "tensor", None),
        P(("parts", "replica"), None, "tensor", None),
        P(None, "tensor", None),
        P(("parts", "replica"), None, None, "tensor"),
        P(("parts", "replica"), None, None, "tensor"),
        P("parts"),
        P("parts", None),
        P("parts", None),
        P("parts"),
        P("parts", None),
        P("parts"),
        P("parts", None),
    )
    out_specs = (
        P(("parts", "replica"), None, "tensor"),
        P(("parts", "replica"), None, "tensor", None),
        P(("parts", "replica"), None, "tensor", None),
        P(("parts", "replica"), None, None, "tensor"),
        P(("parts", "replica"), None, None, "tensor"),
    )
    local = paired if mesh.shape["replica"] == PAIRED else general
    return jax.shard_map(local, mesh=mesh, in_specs=in_specs, out_specs=out_specs, check_vma=False)
```

```python
import functools
import math

import jax
import jax.numpy as jnp
from jax import lax
from jax.experimental import pallas as pl
from jax.experimental.pallas import tpu as pltpu
from jax.sharding import PartitionSpec as P

COPIES = 4


ADAPTER_SCALE = 2.0
ROPE_BASE = 500000.0


def rotate_keys(key_rows, positions):
    head_length = key_rows.shape[-1]
    half_size = head_length // 2
    frequency = ROPE_BASE ** (-(jnp.arange(half_size, dtype=jnp.float32) * 2.0 / head_length))
    angles = positions.astype(jnp.float32)[:, :, None, None] * frequency
    cosine = jnp.cos(angles)
    sine_val = jnp.sin(angles)
    first_half = key_rows[..., :half_size]
    second_half = key_rows[..., half_size:]
    return jnp.concatenate(
        [
            first_half * cosine - second_half * sine_val,
            second_half * cosine + first_half * sine_val,
        ],
        axis=-1,
    )


def attend(queries, stored, lengths_now, fresh_kv):
    request_slot_count, decode_step_count, heads_local, head_length = queries.shape
    local_key_value = stored.shape[2]
    group_size = heads_local // local_key_value
    grouped = queries.reshape(
        request_slot_count, decode_step_count, local_key_value, group_size, head_length
    )
    score_scale = 1.0 / math.sqrt(head_length)
    past_scores = (
        jnp.einsum(
            "msgjd,mcgd->msgjc",
            grouped,
            stored[..., :head_length],
            preferred_element_type=jnp.float32,
        )
        * score_scale
    )
    recent_scores = (
        jnp.einsum(
            "msgjd,mtgd->msgjt",
            grouped,
            fresh_kv[..., :head_length],
            preferred_element_type=jnp.float32,
        )
        * score_scale
    )
    row_ids = jnp.arange(stored.shape[1], dtype=jnp.int32)
    past_ok = (row_ids[None, :] < lengths_now[:, None])[:, None, None, None, :]
    step_ids = jnp.arange(decode_step_count, dtype=jnp.int32)
    recent_ok = (step_ids[None, :] <= step_ids[:, None])[None, :, None, None, :]
    past_scores = jnp.where(past_ok, past_scores, -jnp.inf)
    recent_scores = jnp.where(recent_ok, recent_scores, -jnp.inf)
    peak_score = jnp.maximum(jnp.max(past_scores, -1), jnp.max(recent_scores, -1))[..., None]
    past_exp = jnp.exp(past_scores - peak_score)
    recent_exp = jnp.exp(recent_scores - peak_score)
    denom_sum = jnp.sum(past_exp, -1, keepdims=True) + jnp.sum(recent_exp, -1, keepdims=True)
    past_w = (past_exp / denom_sum).astype(jnp.bfloat16)
    recent_w = (recent_exp / denom_sum).astype(jnp.bfloat16)
    mixed_out = jnp.einsum(
        "msgjc,mcgd->msgjd", past_w, stored[..., head_length:], preferred_element_type=jnp.float32
    )
    mixed_out = mixed_out + jnp.einsum(
        "msgjt,mtgd->msgjd",
        recent_w,
        fresh_kv[..., head_length:],
        preferred_element_type=jnp.float32,
    )
    return mixed_out.reshape(request_slot_count, decode_step_count, heads_local * head_length)


def general(
    hidden,
    queries,
    kv_cache,
    w_kv,
    store_a,
    store_b,
    lengths,
    arrival_from,
    arrival_slot,
    resident_adapter,
    arrival_adapter,
    hot_holder,
    hot_dest,
):
    my_index = lax.axis_index("replica")
    replicas = lax.axis_size("replica")
    resident = kv_cache.shape[0]
    arrive = arrival_from.shape[1]
    request_slot_count = resident + arrive
    decode_step_count = hidden.shape[1]
    head_length = queries.shape[3]
    local_key_value = kv_cache.shape[2]
    slot_total = store_a.shape[0]
    hot_total = hot_holder.shape[0]
    spans = hot_total // COPIES
    my_from = lax.dynamic_index_in_dim(arrival_from, my_index, 0, keepdims=False)
    my_slot = lax.dynamic_index_in_dim(arrival_slot, my_index, 0, keepdims=False)
    own_ids = my_index * resident + jnp.arange(resident, dtype=jnp.int32)
    leaving_ids = (arrival_from * resident + arrival_slot).reshape(-1)
    staying = jnp.logical_not(jnp.any(own_ids[:, None] == leaving_ids[None, :], axis=1))
    live_mask = jnp.concatenate([staying, jnp.ones((arrive,), bool)])
    own_len = lax.dynamic_slice_in_dim(lengths, my_index * resident, resident)
    arrival_len = jnp.take(lengths, my_from * resident + my_slot)
    seen_len = jnp.concatenate([own_len, arrival_len])
    takes_mine = arrival_from == my_index
    sends_any = jnp.any(takes_mine, axis=1)
    send_slot = jnp.sum(jnp.where(takes_mine, arrival_slot, 0), axis=1)
    outgoing = jnp.take(kv_cache, send_slot, axis=0)
    outgoing = jnp.where(sends_any[:, None, None, None], outgoing, jnp.zeros((), jnp.bfloat16))
    incoming = lax.all_to_all(outgoing, "replica", split_axis=0, concat_axis=0, tiled=True)
    blocks = hot_dest.reshape(COPIES, spans, hot_dest.shape[1])
    holder_grid = hot_holder.reshape(COPIES, spans)
    holder_rep = holder_grid // slot_total
    mine = holder_rep == my_index
    has_one = jnp.any(mine, axis=1)
    local_pick = jnp.sum(jnp.where(mine, holder_grid % slot_total, 0), axis=1)

    def spread_rows(store):
        rows = jnp.take(store, local_pick, axis=0)
        rows = jnp.where(has_one[:, None, None, None], rows, jnp.zeros((), jnp.bfloat16))
        return rows.reshape(COPIES, replicas, -1).transpose(1, 0, 2)

    got_a, got_b = (
        lax.all_to_all(spread_rows(store_a), "replica", split_axis=0, concat_axis=0, tiled=True),
        lax.all_to_all(spread_rows(store_b), "replica", split_axis=0, concat_axis=0, tiled=True),
    )
    replica_ids = jnp.arange(replicas, dtype=jnp.int32)
    member = jnp.any(blocks[:, :, :, None] == replica_ids[None, None, None, :], axis=2).astype(
        jnp.int32
    )
    source_rep = jnp.sum(member * holder_rep[:, :, None], axis=1)
    copy_ids = jnp.arange(COPIES, dtype=jnp.int32)
    route_a = got_a[source_rep.T, copy_ids[None, :]]
    route_b = got_b[source_rep.T, copy_ids[None, :]]
    recv_a, recv_b = (
        lax.all_to_all(route_a, "replica", split_axis=0, concat_axis=0, tiled=True),
        lax.all_to_all(route_b, "replica", split_axis=0, concat_axis=0, tiled=True),
    )
    installed_a = recv_a.transpose(1, 0, 2).reshape((COPIES,) + store_a.shape[1:])
    installed_b = recv_b.transpose(1, 0, 2).reshape((COPIES,) + store_b.shape[1:])
    own_adapter = lax.dynamic_slice_in_dim(resident_adapter, my_index * resident, resident)
    my_choice = lax.dynamic_index_in_dim(arrival_adapter, my_index, 0, keepdims=False)
    adapt_a = jnp.concatenate(
        [jnp.take(store_a, own_adapter, axis=0), jnp.take(installed_a, my_choice, axis=0)]
    )
    adapter_up_weight = jnp.concatenate(
        [jnp.take(store_b, own_adapter, axis=0), jnp.take(installed_b, my_choice, axis=0)]
    )
    partial_value = jnp.einsum(
        "msd,mpkd->mspk", hidden, adapt_a, preferred_element_type=jnp.float32
    )
    base_projection = jnp.einsum(
        "msd,dgc->msgc",
        lax.all_gather(hidden, "tensor", axis=2, tiled=True),
        w_kv,
        preferred_element_type=jnp.float32,
    )
    down_projected = lax.psum(partial_value, "tensor")
    down_projected = down_projected.astype(jnp.bfloat16)
    adapter_update = jnp.einsum(
        "gnot,gote->gnoe", down_projected, adapter_up_weight, preferred_element_type=jnp.float32
    )
    adapter_update = (
        adapter_update.reshape(
            request_slot_count, decode_step_count, 2, local_key_value, head_length
        )
        .transpose(0, 1, 3, 2, 4)
        .reshape(request_slot_count, decode_step_count, local_key_value, 2 * head_length)
    )
    unrotated_key_value = base_projection + ADAPTER_SCALE * adapter_update
    positions = seen_len[:, None] + jnp.arange(decode_step_count, dtype=jnp.int32)[None, :]
    fresh_kv = jnp.concatenate(
        [
            rotate_keys(unrotated_key_value[..., :head_length], positions),
            unrotated_key_value[..., head_length:],
        ],
        axis=-1,
    ).astype(jnp.bfloat16)
    stay_out = attend(queries[:resident], kv_cache, own_len, fresh_kv[:resident])
    arrived = jnp.take(incoming, my_from, axis=0)
    row_ids = jnp.arange(kv_cache.shape[1], dtype=jnp.int32)
    arrived = jnp.where(
        (row_ids[None, :] < arrival_len[:, None])[:, :, None, None],
        arrived,
        jnp.zeros((), jnp.bfloat16),
    )
    move_out = attend(queries[resident:], arrived, arrival_len, fresh_kv[resident:])
    mixed_out = jnp.concatenate([stay_out, move_out], axis=0)
    attn_out = jnp.where(live_mask[:, None, None], mixed_out, 0.0).astype(jnp.bfloat16)
    new_kv = jnp.where(live_mask[:, None, None, None], fresh_kv, jnp.zeros((), jnp.bfloat16))
    return (attn_out, new_kv, arrived, installed_a, installed_b)


PAIRED = 4


def needed_first(adapter_ref, dest):
    first, second = adapter_ref[0, dest], adapter_ref[1, dest]
    ids = range(1, COPIES)
    keys = [jnp.where(first == c, 0, jnp.where(second == c, 1, 2 + c)) for c in ids]
    place = [sum(jnp.where(other < key, 1, 0) for other in keys) for key in keys]
    order = [sum(jnp.where(place[c - 1] == j, c, 0) for c in ids) for j in range(COPIES - 1)]
    return order, place


def held_slot(holder_ref, spans, slots, replica, copy_id):
    found = jnp.int32(0)
    for s in range(spans):
        holder = holder_ref[copy_id * spans + s]
        found = jnp.where(holder // slots == replica, holder % slots, found)
    return found


def holder_of(holder_ref, dest_ref, spans, dest, copy_id):
    found = jnp.int32(0)
    for s in range(spans):
        row = copy_id * spans + s
        found = jnp.where(dest_ref[0, row] == dest, holder_ref[row], found)
    return found


class Staged:
    def __init__(self, sems):
        self.sems, self.jobs = sems, []

    def go(self, options, stage, dst):
        sem = self.sems.at[len(self.jobs)]
        for condition, src in options:
            if condition is None:
                pltpu.make_async_copy(src, stage, sem).start()
            else:

                @pl.when(condition)
                def _():
                    pltpu.make_async_copy(src, stage, sem).start()

        self.jobs.append((stage, dst))

    def arrived(self, i):
        stage, _ = self.jobs[i]
        pltpu.make_async_copy(stage, stage, self.sems.at[i]).wait()

    def finish(self):
        half = len(self.jobs)
        for i, (stage, dst) in enumerate(self.jobs):
            self.arrived(i)
            pltpu.make_async_copy(stage, dst, self.sems.at[half + i]).start()
        for i, (stage, dst) in enumerate(self.jobs):
            pltpu.make_async_copy(stage, dst, self.sems.at[half + i]).wait()


def pack_kernel(spans, slots, from_hbm, slot_hbm, adapter_hbm, holder_hbm, a_ref, b_ref, kv_ref,
                z_out, u0_out, u12_out, b_out, k1_out, k2_out, k3_out,
                from_ref, slot_ref, adapter_ref, holder_ref, a_stage, b_stage, k_stage, small_sems, sems):
    me = lax.axis_index("replica")
    small = [
        pltpu.make_async_copy(src, dst, small_sems.at[i])
        for i, (src, dst) in enumerate(
            ((adapter_hbm, adapter_ref), (holder_hbm, holder_ref), (from_hbm, from_ref), (slot_hbm, slot_ref))
        )
    ]
    for copy in small:
        copy.start()
    for copy in small:
        copy.wait()
    staged = Staged(sems)
    order, _ = needed_first(adapter_ref, me ^ 3)
    outs = (z_out, u0_out, u12_out.at[0], u12_out.at[1])
    for j, c in enumerate([0] + order):
        staged.go([(None, a_ref.at[held_slot(holder_ref, spans, slots, me, c)])], a_stage.at[j], outs[j])
        if j == 0:
            for c in range(COPIES):
                staged.go([(None, b_ref.at[held_slot(holder_ref, spans, slots, me, c)])], b_stage.at[c], b_out.at[c])
            for k, out in ((1, k1_out), (2, k2_out), (3, k3_out)):
                chosen = jnp.int32(0)
                for a in range(2):
                    chosen = jnp.where(from_ref[a, me ^ k] == me, slot_ref[a, me ^ k], chosen)
                staged.go([(None, kv_ref.at[chosen])], k_stage.at[k - 1], out)
    staged.finish()


def pick_kernel(spans, slots, places, copies, adapter_ref, holder_ref, dest_ref, a_ref, b_ref, core_a, core_b, *rest):
    outs, (a_stage, b_stage, sems) = rest[:-3], rest[-3:]
    me = lax.axis_index("replica")
    order, _ = needed_first(adapter_ref, me ^ 2)
    staged = Staged(sems)

    def options(c, store, core):
        holder = holder_of(holder_ref, dest_ref, spans, me ^ 2, c)
        mine = holder // slots == me
        return [(mine, store.at[holder % slots]), (jnp.logical_not(mine), core)]

    for i, j in enumerate(places):
        core = core_a if len(core_a.shape) == 3 else core_a.at[i]
        staged.go(options(order[j], a_ref, core), a_stage.at[i], outs[i])
    for c in range(copies):
        staged.go(options(c, b_ref, core_b.at[c]), b_stage.at[c], outs[-1].at[c])
    staged.finish()


def sources(spans, slots, adapter_ref, holder_ref, dest_ref, z_refs, near_refs, far_refs, near_b, far_b):
    me = lax.axis_index("replica")
    _, place_far = needed_first(adapter_ref, me)
    _, place_near = needed_first(adapter_ref, me ^ 2)

    def at(places, c):
        return sum(jnp.where(c == i + 1, place, 0) for i, place in enumerate(places))

    def options(c):
        holder = holder_of(holder_ref, dest_ref, spans, me, c) // slots
        near = holder == (me ^ 1)
        far = jnp.logical_not(near)
        of_a = []
        zero = c == 0
        for k, ref in enumerate(z_refs):
            of_a.append((jnp.logical_and(zero, holder == (me ^ (k + 1))), ref))
        for side, places, refs in ((near, place_near, near_refs), (far, place_far, far_refs)):
            for j, ref in enumerate(refs):
                here = jnp.logical_and(side, at(places, c) == j)
                of_a.append((jnp.logical_and(c != 0, here), ref))
        return of_a, [(near, near_b.at[c]), (far, far_b.at[c])]

    return options


def arrive_kernel(spans, slots, adapter_ref, holder_ref, dest_ref, hid_ref, z1, z2, z3, u0, u12, f0, f1, cb, xb,
                  out_ref, b_out, units, sems):
    me = lax.axis_index("replica")
    options = sources(
        spans, slots, adapter_ref, holder_ref, dest_ref, (z1, z2, z3), (u0, u12.at[0], u12.at[1]), (f0, f1), cb, xb
    )
    staged = Staged(sems)
    for a in range(2):
        of_a, of_b = options(adapter_ref[a, me])
        staged.go(of_a, units.at[a], None)
        staged.go(of_b, b_out.at[a], None)
    for a in range(2):
        staged.arrived(2 * a)
        unit = units[a].reshape(units.shape[1] * units.shape[2], units.shape[3])
        out_ref[a] = lax.dot_general(hid_ref[...], unit, (((1,), (1,)), ((), ())), preferred_element_type=jnp.float32)
        staged.arrived(2 * a + 1)


def install_kernel(spans, slots, adapter_ref, holder_ref, dest_ref, z1, z2, z3, u0, u12, f0, f1, f2, cb, xb,
                   a_out, b_out, a_stage, b_stage, sems):
    options = sources(
        spans, slots, adapter_ref, holder_ref, dest_ref, (z1, z2, z3), (u0, u12.at[0], u12.at[1]), (f0, f1, f2), cb, xb
    )
    staged = Staged(sems)
    for c in range(COPIES):
        of_a, of_b = options(jnp.int32(c))
        staged.go(of_a, a_stage.at[c], a_out.at[c])
        staged.go(of_b, b_stage.at[c], b_out.at[c])
    staged.finish()


SMEM = pl.BlockSpec(memory_space=pltpu.SMEM)
ANY = pl.BlockSpec(memory_space=pl.ANY)
VMEM = pl.BlockSpec(memory_space=pltpu.VMEM)


def paired(
    hidden,
    queries,
    kv_cache,
    w_kv,
    store_a,
    store_b,
    lengths,
    arrival_from,
    arrival_slot,
    resident_adapter,
    arrival_adapter,
    hot_holder,
    hot_dest,
):
    me = lax.axis_index("replica")
    tensors = lax.axis_size("tensor")
    tensor_index = lax.axis_index("tensor")
    resident, arrive = kv_cache.shape[0], arrival_from.shape[1]
    requests, steps, width = hidden.shape
    head_length, heads = queries.shape[3], kv_cache.shape[2]
    slots = store_a.shape[0]
    spans = hot_holder.shape[0] // COPIES
    kind = store_a.dtype
    unit_a, unit_b, unit_k = store_a.shape[1:], store_b.shape[1:], kv_cache.shape[1:]

    def shaped(*shape, dtype=kind):
        return jax.ShapeDtypeStruct(shape, dtype)

    def swap(array, k):
        return lax.ppermute(array, "replica", [(i, i ^ k) for i in range(PAIRED)])

    def shift(array, k):
        return lax.ppermute(array, "tensor", [(i, (i + k) % tensors) for i in range(tensors)])

    def cost(bytes_accessed, flops=0):
        return pl.CostEstimate(flops=flops, bytes_accessed=bytes_accessed, transcendentals=0)

    size_a, size_b = 2 * math.prod(unit_a), 2 * math.prod(unit_b)

    plan = (arrival_adapter.T, hot_holder, hot_dest.T)
    leave = (arrival_from.T, arrival_slot.T)

    z, u0, u12, b_all, k1, k2, k3 = pl.pallas_call(
        functools.partial(pack_kernel, spans, slots),
        out_shape=(
            shaped(*unit_a), shaped(*unit_a), shaped(2, *unit_a), shaped(COPIES, *unit_b),
            shaped(*unit_k), shaped(*unit_k), shaped(*unit_k),
        ),
        in_specs=[ANY] * 7,
        out_specs=(ANY,) * 7,
        scratch_shapes=[pltpu.SMEM(x.shape, x.dtype) for x in leave + plan[:2]]
        + [
            pltpu.VMEM((COPIES,) + unit_a, kind),
            pltpu.VMEM((COPIES,) + unit_b, kind),
            pltpu.VMEM((3,) + unit_k, kind),
            pltpu.SemaphoreType.DMA((4,)),
            pltpu.SemaphoreType.DMA((2 * (2 * COPIES + 3),)),
        ],
        cost_estimate=cost(8 * size_a + 8 * size_b),
    )(*leave, *plan[:2], store_a, store_b, kv_cache)
    z2 = swap(z, 2)
    core_u0, core_b = swap(u0, 1), swap(b_all, 1)
    core_u12 = swap(u12, 1)
    u0, hidden = lax.optimization_barrier((u0, hidden))

    def pick(places, copies, core):
        out = pl.pallas_call(
            functools.partial(pick_kernel, spans, slots, places, copies),
            out_shape=tuple(shaped(*unit_a) for _ in places) + (shaped(COPIES, *unit_b),) * (copies > 0),
            in_specs=[SMEM] * 3 + [ANY] * 4,
            out_specs=(ANY,) * (len(places) + (copies > 0)),
            scratch_shapes=[
                pltpu.VMEM((len(places),) + unit_a, kind),
                pltpu.VMEM((COPIES,) + unit_b, kind),
                pltpu.SemaphoreType.DMA((2 * (len(places) + copies),)),
            ],
            cost_estimate=cost(2 * len(places) * size_a + 2 * copies * size_b),
        )(*plan, store_a, store_b, core, core_b)
        return out

    to0, to_b = pick((0,), COPIES, core_u0)
    f0 = swap(to0, 2)
    to1, to2 = pick((1, 2), 0, core_u12)

    z2, to1 = lax.optimization_barrier((z2, to1))
    f1 = swap(to1, 2)
    f0, to_b, k2, k3 = lax.optimization_barrier((f0, to_b, k2, k3))
    far_b = swap(to_b, 2)
    far = (swap(k2, 2), swap(k3, 3))
    far_b, to2 = lax.optimization_barrier((far_b, to2))
    f2 = swap(to2, 2)

    own_adapter = lax.dynamic_slice_in_dim(resident_adapter, me * resident, resident)
    every = jnp.einsum("msd,epkd->msepk", hidden[:resident], store_a, preferred_element_type=jnp.float32)
    is_own = own_adapter[:, None] == jnp.arange(slots, dtype=jnp.int32)[None, :]
    part_own = jnp.sum(jnp.where(is_own[:, None, :, None, None], every, 0.0), axis=2)

    _, part_own = lax.optimization_barrier((to0, part_own))

    def total(part):
        out = part
        for k in range(1, tensors):
            out = out + shift(part, k)
        return out.astype(jnp.bfloat16)

    shrink_own = total(part_own.reshape(resident * steps, -1)).reshape(resident, steps, 2, -1)
    _, _, _, shrink_own, hidden, lengths, kv_cache, queries = lax.optimization_barrier(
        (to1, to2, z2, shrink_own, hidden, lengths, kv_cache, queries)
    )
    pieces = [hidden] + [shift(hidden, k) for k in range(1, tensors)]
    pieces, z, k1 = lax.optimization_barrier((pieces, z, k1))
    z1, z3, near = swap(z, 1), swap(z2, 1), swap(k1, 1)
    whole = jnp.concatenate(pieces, axis=2)
    whole = whole.reshape(requests, steps, tensors, width)
    turn = (tensor_index - jnp.arange(tensors, dtype=jnp.int32)) % tensors
    whole = jnp.take(whole, turn, axis=2).reshape(requests, steps, tensors * width)
    base = jnp.einsum("msd,dgc->msgc", whole, w_kv, preferred_element_type=jnp.float32)

    my_from = lax.dynamic_index_in_dim(arrival_from, me, 0, keepdims=False)
    my_slot = lax.dynamic_index_in_dim(arrival_slot, me, 0, keepdims=False)
    own_ids = me * resident + jnp.arange(resident, dtype=jnp.int32)
    leaving = (arrival_from * resident + arrival_slot).reshape(-1)
    staying = jnp.logical_not(jnp.any(own_ids[:, None] == leaving[None, :], axis=1))
    own_len = lax.dynamic_slice_in_dim(lengths, me * resident, resident)
    arrival_len = jnp.take(lengths, my_from * resident + my_slot)

    def fresh_rows(base_rows, shrink, up, seen):
        count = base_rows.shape[0]
        update = jnp.einsum("gnot,gote->gnoe", shrink, up, preferred_element_type=jnp.float32)
        update = update.reshape(count, steps, 2, heads, head_length).transpose(0, 1, 3, 2, 4)
        raw = base_rows + ADAPTER_SCALE * update.reshape(count, steps, heads, 2 * head_length)
        positions = seen[:, None] + jnp.arange(steps, dtype=jnp.int32)[None, :]
        turned = rotate_keys(raw[..., :head_length], positions)
        return jnp.concatenate([turned, raw[..., head_length:]], axis=-1).astype(jnp.bfloat16)

    up_own = jnp.take(store_b, own_adapter, axis=0)
    fresh_own = fresh_rows(base[:resident], shrink_own, up_own, own_len)
    stay_out = attend(queries[:resident], kv_cache, own_len, fresh_own)
    stay_out = jnp.where(staying[:, None, None], stay_out, 0.0).astype(jnp.bfloat16)
    stay_kv = jnp.where(staying[:, None, None, None], fresh_own, jnp.zeros((), jnp.bfloat16))

    way = (my_from ^ me)[:, None, None, None]
    arrived = jnp.where(way == 1, near[None], jnp.where(way == 2, far[0][None], far[1][None]))
    row_ids = jnp.arange(kv_cache.shape[1], dtype=jnp.int32)
    arrived = jnp.where((row_ids[None, :] < arrival_len[:, None])[:, :, None, None], arrived, jnp.zeros((), jnp.bfloat16))
    rows = 16
    guests = jnp.pad(hidden[resident:].reshape(arrive * steps, width), ((0, rows - arrive * steps), (0, 0)))
    part_new, up_new = pl.pallas_call(
        functools.partial(arrive_kernel, spans, slots),
        out_shape=(shaped(arrive, rows, math.prod(unit_a[:2]), dtype=jnp.float32), shaped(arrive, *unit_b)),
        in_specs=[SMEM] * 3 + [VMEM] + [ANY] * 9,
        out_specs=(VMEM, VMEM),
        scratch_shapes=[pltpu.VMEM((arrive,) + unit_a, kind), pltpu.SemaphoreType.DMA((2 * arrive,))],
        cost_estimate=cost(arrive * (size_a + 2 * size_b), 2 * arrive * rows * size_a // 2),
    )(*plan, guests, z1, z2, z3, core_u0, core_u12, f0, f1, core_b, far_b)
    part_new = jnp.concatenate([part_new[a, a * steps : (a + 1) * steps] for a in range(arrive)], axis=0)
    shrink_new = total(part_new).reshape(arrive, steps, 2, -1)
    fresh_new = fresh_rows(base[resident:], shrink_new, up_new, arrival_len)
    move_out = attend(queries[resident:], arrived, arrival_len, fresh_new).astype(jnp.bfloat16)

    attn_out = jnp.concatenate([stay_out, move_out], axis=0)
    new_kv = jnp.concatenate([stay_kv, fresh_new], axis=0)
    installed_a, installed_b = pl.pallas_call(
        functools.partial(install_kernel, spans, slots),
        out_shape=(shaped(COPIES, *unit_a), shaped(COPIES, *unit_b)),
        in_specs=[SMEM] * 3 + [ANY] * 10,
        out_specs=(ANY, ANY),
        scratch_shapes=[
            pltpu.VMEM((COPIES,) + unit_a, kind),
            pltpu.VMEM((COPIES,) + unit_b, kind),
            pltpu.SemaphoreType.DMA((4 * COPIES,)),
        ],
        cost_estimate=cost(8 * size_a + 8 * size_b),
    )(*plan, z1, z2, z3, core_u0, core_u12, f0, f1, f2, core_b, far_b)
    return (attn_out, new_kv, arrived, installed_a, installed_b)


def solution(mesh):
    in_specs = (
        P(("parts", "replica"), None, "tensor"),
        P(("parts", "replica"), None, "tensor", None),
        P(("parts", "replica"), None, "tensor", None),
        P(None, "tensor", None),
        P(("parts", "replica"), None, None, "tensor"),
        P(("parts", "replica"), None, None, "tensor"),
        P("parts"),
        P("parts", None),
        P("parts", None),
        P("parts"),
        P("parts", None),
        P("parts"),
        P("parts", None),
    )
    out_specs = (
        P(("parts", "replica"), None, "tensor"),
        P(("parts", "replica"), None, "tensor", None),
        P(("parts", "replica"), None, "tensor", None),
        P(("parts", "replica"), None, None, "tensor"),
        P(("parts", "replica"), None, None, "tensor"),
    )
    local = paired if mesh.shape["replica"] == PAIRED else general
    return jax.shard_map(local, mesh=mesh, in_specs=in_specs, out_specs=out_specs, check_vma=False)
```

```python
import functools
import math

import jax
import jax.numpy as jnp
from jax import lax
from jax.experimental import pallas as pl
from jax.experimental.pallas import tpu as pltpu
from jax.sharding import PartitionSpec as P

COPIES = 4


ADAPTER_SCALE = 2.0
ROPE_BASE = 500000.0


def rotate_keys(key_rows, positions):
    head_length = key_rows.shape[-1]
    half_size = head_length // 2
    frequency = ROPE_BASE ** (-(jnp.arange(half_size, dtype=jnp.float32) * 2.0 / head_length))
    angles = positions.astype(jnp.float32)[:, :, None, None] * frequency
    cosine = jnp.cos(angles)
    sine_val = jnp.sin(angles)
    first_half = key_rows[..., :half_size]
    second_half = key_rows[..., half_size:]
    return jnp.concatenate(
        [
            first_half * cosine - second_half * sine_val,
            second_half * cosine + first_half * sine_val,
        ],
        axis=-1,
    )


def attend(queries, stored, lengths_now, fresh_kv):
    request_slot_count, decode_step_count, heads_local, head_length = queries.shape
    local_key_value = stored.shape[2]
    group_size = heads_local // local_key_value
    grouped = queries.reshape(
        request_slot_count, decode_step_count, local_key_value, group_size, head_length
    )
    score_scale = 1.0 / math.sqrt(head_length)
    past_scores = (
        jnp.einsum(
            "msgjd,mcgd->msgjc",
            grouped,
            stored[..., :head_length],
            preferred_element_type=jnp.float32,
        )
        * score_scale
    )
    recent_scores = (
        jnp.einsum(
            "msgjd,mtgd->msgjt",
            grouped,
            fresh_kv[..., :head_length],
            preferred_element_type=jnp.float32,
        )
        * score_scale
    )
    row_ids = jnp.arange(stored.shape[1], dtype=jnp.int32)
    past_ok = (row_ids[None, :] < lengths_now[:, None])[:, None, None, None, :]
    step_ids = jnp.arange(decode_step_count, dtype=jnp.int32)
    recent_ok = (step_ids[None, :] <= step_ids[:, None])[None, :, None, None, :]
    past_scores = jnp.where(past_ok, past_scores, -jnp.inf)
    recent_scores = jnp.where(recent_ok, recent_scores, -jnp.inf)
    peak_score = jnp.maximum(jnp.max(past_scores, -1), jnp.max(recent_scores, -1))[..., None]
    past_exp = jnp.exp(past_scores - peak_score)
    recent_exp = jnp.exp(recent_scores - peak_score)
    denom_sum = jnp.sum(past_exp, -1, keepdims=True) + jnp.sum(recent_exp, -1, keepdims=True)
    past_w = (past_exp / denom_sum).astype(jnp.bfloat16)
    recent_w = (recent_exp / denom_sum).astype(jnp.bfloat16)
    mixed_out = jnp.einsum(
        "msgjc,mcgd->msgjd", past_w, stored[..., head_length:], preferred_element_type=jnp.float32
    )
    mixed_out = mixed_out + jnp.einsum(
        "msgjt,mtgd->msgjd",
        recent_w,
        fresh_kv[..., head_length:],
        preferred_element_type=jnp.float32,
    )
    return mixed_out.reshape(request_slot_count, decode_step_count, heads_local * head_length)


def general(
    hidden,
    queries,
    kv_cache,
    w_kv,
    store_a,
    store_b,
    lengths,
    arrival_from,
    arrival_slot,
    resident_adapter,
    arrival_adapter,
    hot_holder,
    hot_dest,
):
    my_index = lax.axis_index("replica")
    replicas = lax.axis_size("replica")
    resident = kv_cache.shape[0]
    arrive = arrival_from.shape[1]
    request_slot_count = resident + arrive
    decode_step_count = hidden.shape[1]
    head_length = queries.shape[3]
    local_key_value = kv_cache.shape[2]
    slot_total = store_a.shape[0]
    hot_total = hot_holder.shape[0]
    spans = hot_total // COPIES
    my_from = lax.dynamic_index_in_dim(arrival_from, my_index, 0, keepdims=False)
    my_slot = lax.dynamic_index_in_dim(arrival_slot, my_index, 0, keepdims=False)
    own_ids = my_index * resident + jnp.arange(resident, dtype=jnp.int32)
    leaving_ids = (arrival_from * resident + arrival_slot).reshape(-1)
    staying = jnp.logical_not(jnp.any(own_ids[:, None] == leaving_ids[None, :], axis=1))
    live_mask = jnp.concatenate([staying, jnp.ones((arrive,), bool)])
    own_len = lax.dynamic_slice_in_dim(lengths, my_index * resident, resident)
    arrival_len = jnp.take(lengths, my_from * resident + my_slot)
    seen_len = jnp.concatenate([own_len, arrival_len])
    takes_mine = arrival_from == my_index
    sends_any = jnp.any(takes_mine, axis=1)
    send_slot = jnp.sum(jnp.where(takes_mine, arrival_slot, 0), axis=1)
    outgoing = jnp.take(kv_cache, send_slot, axis=0)
    outgoing = jnp.where(sends_any[:, None, None, None], outgoing, jnp.zeros((), jnp.bfloat16))
    incoming = lax.all_to_all(outgoing, "replica", split_axis=0, concat_axis=0, tiled=True)
    blocks = hot_dest.reshape(COPIES, spans, hot_dest.shape[1])
    holder_grid = hot_holder.reshape(COPIES, spans)
    holder_rep = holder_grid // slot_total
    mine = holder_rep == my_index
    has_one = jnp.any(mine, axis=1)
    local_pick = jnp.sum(jnp.where(mine, holder_grid % slot_total, 0), axis=1)

    def spread_rows(store):
        rows = jnp.take(store, local_pick, axis=0)
        rows = jnp.where(has_one[:, None, None, None], rows, jnp.zeros((), jnp.bfloat16))
        return rows.reshape(COPIES, replicas, -1).transpose(1, 0, 2)

    got_a, got_b = (
        lax.all_to_all(spread_rows(store_a), "replica", split_axis=0, concat_axis=0, tiled=True),
        lax.all_to_all(spread_rows(store_b), "replica", split_axis=0, concat_axis=0, tiled=True),
    )
    replica_ids = jnp.arange(replicas, dtype=jnp.int32)
    member = jnp.any(blocks[:, :, :, None] == replica_ids[None, None, None, :], axis=2).astype(
        jnp.int32
    )
    source_rep = jnp.sum(member * holder_rep[:, :, None], axis=1)
    copy_ids = jnp.arange(COPIES, dtype=jnp.int32)
    route_a = got_a[source_rep.T, copy_ids[None, :]]
    route_b = got_b[source_rep.T, copy_ids[None, :]]
    recv_a, recv_b = (
        lax.all_to_all(route_a, "replica", split_axis=0, concat_axis=0, tiled=True),
        lax.all_to_all(route_b, "replica", split_axis=0, concat_axis=0, tiled=True),
    )
    installed_a = recv_a.transpose(1, 0, 2).reshape((COPIES,) + store_a.shape[1:])
    installed_b = recv_b.transpose(1, 0, 2).reshape((COPIES,) + store_b.shape[1:])
    own_adapter = lax.dynamic_slice_in_dim(resident_adapter, my_index * resident, resident)
    my_choice = lax.dynamic_index_in_dim(arrival_adapter, my_index, 0, keepdims=False)
    adapt_a = jnp.concatenate(
        [jnp.take(store_a, own_adapter, axis=0), jnp.take(installed_a, my_choice, axis=0)]
    )
    adapter_up_weight = jnp.concatenate(
        [jnp.take(store_b, own_adapter, axis=0), jnp.take(installed_b, my_choice, axis=0)]
    )
    partial_value = jnp.einsum(
        "msd,mpkd->mspk", hidden, adapt_a, preferred_element_type=jnp.float32
    )
    base_projection = jnp.einsum(
        "msd,dgc->msgc",
        lax.all_gather(hidden, "tensor", axis=2, tiled=True),
        w_kv,
        preferred_element_type=jnp.float32,
    )
    down_projected = lax.psum(partial_value, "tensor")
    down_projected = down_projected.astype(jnp.bfloat16)
    adapter_update = jnp.einsum(
        "gnot,gote->gnoe", down_projected, adapter_up_weight, preferred_element_type=jnp.float32
    )
    adapter_update = (
        adapter_update.reshape(
            request_slot_count, decode_step_count, 2, local_key_value, head_length
        )
        .transpose(0, 1, 3, 2, 4)
        .reshape(request_slot_count, decode_step_count, local_key_value, 2 * head_length)
    )
    unrotated_key_value = base_projection + ADAPTER_SCALE * adapter_update
    positions = seen_len[:, None] + jnp.arange(decode_step_count, dtype=jnp.int32)[None, :]
    fresh_kv = jnp.concatenate(
        [
            rotate_keys(unrotated_key_value[..., :head_length], positions),
            unrotated_key_value[..., head_length:],
        ],
        axis=-1,
    ).astype(jnp.bfloat16)
    stay_out = attend(queries[:resident], kv_cache, own_len, fresh_kv[:resident])
    arrived = jnp.take(incoming, my_from, axis=0)
    row_ids = jnp.arange(kv_cache.shape[1], dtype=jnp.int32)
    arrived = jnp.where(
        (row_ids[None, :] < arrival_len[:, None])[:, :, None, None],
        arrived,
        jnp.zeros((), jnp.bfloat16),
    )
    move_out = attend(queries[resident:], arrived, arrival_len, fresh_kv[resident:])
    mixed_out = jnp.concatenate([stay_out, move_out], axis=0)
    attn_out = jnp.where(live_mask[:, None, None], mixed_out, 0.0).astype(jnp.bfloat16)
    new_kv = jnp.where(live_mask[:, None, None, None], fresh_kv, jnp.zeros((), jnp.bfloat16))
    return (attn_out, new_kv, arrived, installed_a, installed_b)


PAIRED = 4
TENSORS = 4


def needed_first(adapter_ref, dest):
    first, second = adapter_ref[0, dest], adapter_ref[1, dest]
    ids = range(1, COPIES)
    keys = [jnp.where(first == c, 0, jnp.where(second == c, 1, 2 + c)) for c in ids]
    place = [sum(jnp.where(other < key, 1, 0) for other in keys) for key in keys]
    order = [sum(jnp.where(place[c - 1] == j, c, 0) for c in ids) for j in range(COPIES - 1)]
    return order, place


def held_slot(holder_ref, spans, slots, replica, copy_id):
    found = jnp.int32(0)
    for s in range(spans):
        holder = holder_ref[copy_id * spans + s]
        found = jnp.where(holder // slots == replica, holder % slots, found)
    return found


def holder_of(holder_ref, dest_ref, spans, dest, copy_id):
    found = jnp.int32(0)
    for s in range(spans):
        row = copy_id * spans + s
        found = jnp.where(dest_ref[0, row] == dest, holder_ref[row], found)
    return found


class Staged:
    def __init__(self, sems):
        self.sems, self.jobs = sems, []

    def go(self, options, stage, dst):
        sem = self.sems.at[len(self.jobs)]
        for condition, src in options:
            if condition is None:
                pltpu.make_async_copy(src, stage, sem).start()
            else:

                @pl.when(condition)
                def _():
                    pltpu.make_async_copy(src, stage, sem).start()

        self.jobs.append((stage, dst))

    def arrived(self, i):
        stage, _ = self.jobs[i]
        pltpu.make_async_copy(stage, stage, self.sems.at[i]).wait()

    def finish(self):
        half = len(self.jobs)
        for i, (stage, dst) in enumerate(self.jobs):
            self.arrived(i)
            pltpu.make_async_copy(stage, dst, self.sems.at[half + i]).start()
        for i, (stage, dst) in enumerate(self.jobs):
            pltpu.make_async_copy(stage, dst, self.sems.at[half + i]).wait()


def pack_kernel(spans, slots, from_hbm, slot_hbm, adapter_hbm, holder_hbm, a_ref, b_ref, kv_ref,
                z_out, u_out, b_out, k1_out, k2_out, k3_out,
                from_ref, slot_ref, adapter_ref, holder_ref, a_stage, b_stage, k_stage, small_sems, sems):
    me = lax.axis_index("replica")
    small = [
        pltpu.make_async_copy(src, dst, small_sems.at[i])
        for i, (src, dst) in enumerate(
            ((adapter_hbm, adapter_ref), (holder_hbm, holder_ref), (from_hbm, from_ref), (slot_hbm, slot_ref))
        )
    ]
    for copy in small:
        copy.start()
    for copy in small:
        copy.wait()
    staged = Staged(sems)
    order, _ = needed_first(adapter_ref, me ^ 3)
    outs = [z_out] + [u_out.at[j] for j in range(COPIES - 1)]
    for j, c in enumerate([0] + order):
        staged.go([(None, a_ref.at[held_slot(holder_ref, spans, slots, me, c)])], a_stage.at[j], outs[j])
        if j == 0:
            for c in range(COPIES):
                staged.go([(None, b_ref.at[held_slot(holder_ref, spans, slots, me, c)])], b_stage.at[c], b_out.at[c])
            for k, out in ((1, k1_out), (2, k2_out), (3, k3_out)):
                chosen = jnp.int32(0)
                for a in range(2):
                    chosen = jnp.where(from_ref[a, me ^ k] == me, slot_ref[a, me ^ k], chosen)
                staged.go([(None, kv_ref.at[chosen])], k_stage.at[k - 1], out)
    staged.finish()


def pick_kernel(spans, slots, places, copies, adapter_ref, holder_ref, dest_ref, a_ref, b_ref, core_a, core_b, *rest):
    outs, (a_stage, b_stage, sems) = rest[:-3], rest[-3:]
    me = lax.axis_index("replica")
    order, _ = needed_first(adapter_ref, me ^ 2)
    staged = Staged(sems)

    def options(c, store, core):
        holder = holder_of(holder_ref, dest_ref, spans, me ^ 2, c)
        mine = holder // slots == me
        return [(mine, store.at[holder % slots]), (jnp.logical_not(mine), core)]

    for i, j in enumerate(places):
        staged.go(options(order[j], a_ref, core_a.at[j]), a_stage.at[i], outs[i])
    for c in range(copies):
        staged.go(options(c, b_ref, core_b.at[c]), b_stage.at[c], outs[-1].at[c])
    staged.finish()


def sources(spans, slots, adapter_ref, holder_ref, dest_ref, z_refs, near_refs, far_refs, near_b, far_b):
    me = lax.axis_index("replica")
    _, place_far = needed_first(adapter_ref, me)
    _, place_near = needed_first(adapter_ref, me ^ 2)

    def at(places, c):
        return sum(jnp.where(c == i + 1, place, 0) for i, place in enumerate(places))

    def options(c):
        holder = holder_of(holder_ref, dest_ref, spans, me, c) // slots
        near = holder == (me ^ 1)
        far = jnp.logical_not(near)
        of_a = []
        zero = c == 0
        for k, ref in enumerate(z_refs):
            of_a.append((jnp.logical_and(zero, holder == (me ^ (k + 1))), ref))
        for side, places, refs in ((near, place_near, near_refs), (far, place_far, far_refs)):
            for j, ref in enumerate(refs):
                here = jnp.logical_and(side, at(places, c) == j)
                of_a.append((jnp.logical_and(c != 0, here), ref))
        return of_a, [(near, near_b.at[c]), (far, far_b.at[c])]

    return options


def arrive_kernel(spans, slots, adapter_ref, holder_ref, dest_ref, hid_ref, z1, z2, z3, u, f0, f1, cb, xb,
                  out_ref, b_out, units, sems):
    me = lax.axis_index("replica")
    options = sources(
        spans, slots, adapter_ref, holder_ref, dest_ref, (z1, z2, z3), [u.at[j] for j in range(COPIES - 1)], (f0, f1), cb, xb
    )
    staged = Staged(sems)
    for a in range(2):
        of_a, of_b = options(adapter_ref[a, me])
        staged.go(of_a, units.at[a], None)
        staged.go(of_b, b_out.at[a], None)
    for a in range(2):
        staged.arrived(2 * a)
        unit = units[a].reshape(units.shape[1] * units.shape[2], units.shape[3])
        out_ref[a] = lax.dot_general(hid_ref[...], unit, (((1,), (1,)), ((), ())), preferred_element_type=jnp.float32)
        staged.arrived(2 * a + 1)


def install_kernel(spans, slots, adapter_ref, holder_ref, dest_ref, z1, z2, z3, u, f0, f1, f2, cb, xb,
                   a_out, b_out, a_stage, b_stage, sems):
    options = sources(
        spans, slots, adapter_ref, holder_ref, dest_ref, (z1, z2, z3), [u.at[j] for j in range(COPIES - 1)], (f0, f1, f2), cb, xb
    )
    staged = Staged(sems)
    for c in range(COPIES):
        of_a, of_b = options(jnp.int32(c))
        staged.go(of_a, a_stage.at[c], a_out.at[c])
        staged.go(of_b, b_stage.at[c], b_out.at[c])
    staged.finish()


SMEM = pl.BlockSpec(memory_space=pltpu.SMEM)
ANY = pl.BlockSpec(memory_space=pl.ANY)
VMEM = pl.BlockSpec(memory_space=pltpu.VMEM)


def paired(
    hidden,
    queries,
    kv_cache,
    w_kv,
    store_a,
    store_b,
    lengths,
    arrival_from,
    arrival_slot,
    resident_adapter,
    arrival_adapter,
    hot_holder,
    hot_dest,
):
    me = lax.axis_index("replica")
    tensor_index = lax.axis_index("tensor")
    resident, arrive = kv_cache.shape[0], arrival_from.shape[1]
    requests, steps, width = hidden.shape
    head_length, heads = queries.shape[3], kv_cache.shape[2]
    slots = store_a.shape[0]
    spans = hot_holder.shape[0] // COPIES
    kind = store_a.dtype
    unit_a, unit_b, unit_k = store_a.shape[1:], store_b.shape[1:], kv_cache.shape[1:]

    def shaped(*shape, dtype=kind):
        return jax.ShapeDtypeStruct(shape, dtype)

    def swap(array, k):
        return lax.ppermute(array, "replica", [(i, i ^ k) for i in range(PAIRED)])

    def mirror(array, k):
        return lax.ppermute(array, "tensor", [(i, i ^ k) for i in range(TENSORS)])

    def cost(bytes_accessed, flops=0):
        return pl.CostEstimate(flops=flops, bytes_accessed=bytes_accessed, transcendentals=0)

    size_a, size_b = 2 * math.prod(unit_a), 2 * math.prod(unit_b)

    plan = (arrival_adapter.T, hot_holder, hot_dest.T)
    leave = (arrival_from.T, arrival_slot.T)

    z, u, b_all, k1, k2, k3 = pl.pallas_call(
        functools.partial(pack_kernel, spans, slots),
        out_shape=(
            shaped(*unit_a), shaped(COPIES - 1, *unit_a), shaped(COPIES, *unit_b),
            shaped(*unit_k), shaped(*unit_k), shaped(*unit_k),
        ),
        in_specs=[ANY] * 7,
        out_specs=(ANY,) * 6,
        scratch_shapes=[pltpu.SMEM(x.shape, x.dtype) for x in leave + plan[:2]]
        + [
            pltpu.VMEM((COPIES,) + unit_a, kind),
            pltpu.VMEM((COPIES,) + unit_b, kind),
            pltpu.VMEM((3,) + unit_k, kind),
            pltpu.SemaphoreType.DMA((4,)),
            pltpu.SemaphoreType.DMA((2 * (2 * COPIES + 3),)),
        ],
        cost_estimate=cost(8 * size_a + 8 * size_b),
    )(*leave, *plan[:2], store_a, store_b, kv_cache)
    z2 = swap(z, 2)
    core_u, core_b = swap(u, 1), swap(b_all, 1)
    far = (swap(k2, 2), swap(k3, 3))

    u, hidden = lax.optimization_barrier((u, hidden))
    own_adapter = lax.dynamic_slice_in_dim(resident_adapter, me * resident, resident)
    every = jnp.einsum("msd,epkd->msepk", hidden[:resident], store_a, preferred_element_type=jnp.float32)
    is_own = own_adapter[:, None] == jnp.arange(slots, dtype=jnp.int32)[None, :]
    part_own = jnp.sum(jnp.where(is_own[:, None, :, None, None], every, 0.0), axis=2)
    part_own, core_u = lax.optimization_barrier((part_own, core_u))

    def pick(places, copies, core):
        out = pl.pallas_call(
            functools.partial(pick_kernel, spans, slots, places, copies),
            out_shape=tuple(shaped(*unit_a) for _ in places) + (shaped(COPIES, *unit_b),) * (copies > 0),
            in_specs=[SMEM] * 3 + [ANY] * 4,
            out_specs=(ANY,) * (len(places) + (copies > 0)),
            scratch_shapes=[
                pltpu.VMEM((len(places),) + unit_a, kind),
                pltpu.VMEM((COPIES,) + unit_b, kind),
                pltpu.SemaphoreType.DMA((2 * (len(places) + copies),)),
            ],
            cost_estimate=cost(2 * len(places) * size_a + 2 * copies * size_b),
        )(*plan, store_a, store_b, core, core_b)
        return out

    to0, to1, to2, to_b = pick((0, 1, 2), COPIES, core_u)
    f0 = swap(to0, 2)

    z2, far, to1, to_b = lax.optimization_barrier((z2, far, to1, to_b))
    f1, far_b = swap(to1, 2), swap(to_b, 2)

    _, part_own, hidden, lengths, kv_cache, queries = lax.optimization_barrier(
        (to0, part_own, hidden, lengths, kv_cache, queries)
    )

    def total(part):
        out = part
        for k in (2, 1):
            out = out + mirror(out, k)
        return out.astype(jnp.bfloat16)

    shrink_own = total(part_own.reshape(resident * steps, -1)).reshape(resident, steps, 2, -1)
    high, low = tensor_index >= 2, tensor_index % 2 == 1
    other = mirror(hidden, 2)
    halves = jnp.concatenate([jnp.where(high, other, hidden), jnp.where(high, hidden, other)], axis=2)
    other = mirror(halves, 1)
    even, odd = jnp.where(low, other, halves), jnp.where(low, halves, other)
    whole = jnp.concatenate([even[..., :width], odd[..., :width], even[..., width:], odd[..., width:]], axis=2)
    f0, whole, to2, z, k1 = lax.optimization_barrier((f0, whole, to2, z, k1))
    f2 = swap(to2, 2)
    z1, z3, near = swap(z, 1), swap(z2, 1), swap(k1, 1)
    base = jnp.einsum("msd,dgc->msgc", whole, w_kv, preferred_element_type=jnp.float32)

    my_from = lax.dynamic_index_in_dim(arrival_from, me, 0, keepdims=False)
    my_slot = lax.dynamic_index_in_dim(arrival_slot, me, 0, keepdims=False)
    own_ids = me * resident + jnp.arange(resident, dtype=jnp.int32)
    leaving = (arrival_from * resident + arrival_slot).reshape(-1)
    staying = jnp.logical_not(jnp.any(own_ids[:, None] == leaving[None, :], axis=1))
    own_len = lax.dynamic_slice_in_dim(lengths, me * resident, resident)
    arrival_len = jnp.take(lengths, my_from * resident + my_slot)

    def fresh_rows(base_rows, shrink, up, seen):
        count = base_rows.shape[0]
        update = jnp.einsum("gnot,gote->gnoe", shrink, up, preferred_element_type=jnp.float32)
        update = update.reshape(count, steps, 2, heads, head_length).transpose(0, 1, 3, 2, 4)
        raw = base_rows + ADAPTER_SCALE * update.reshape(count, steps, heads, 2 * head_length)
        positions = seen[:, None] + jnp.arange(steps, dtype=jnp.int32)[None, :]
        turned = rotate_keys(raw[..., :head_length], positions)
        return jnp.concatenate([turned, raw[..., head_length:]], axis=-1).astype(jnp.bfloat16)

    up_own = jnp.take(store_b, own_adapter, axis=0)
    fresh_own = fresh_rows(base[:resident], shrink_own, up_own, own_len)
    stay_out = attend(queries[:resident], kv_cache, own_len, fresh_own)
    stay_out = jnp.where(staying[:, None, None], stay_out, 0.0).astype(jnp.bfloat16)
    stay_kv = jnp.where(staying[:, None, None, None], fresh_own, jnp.zeros((), jnp.bfloat16))

    way = (my_from ^ me)[:, None, None, None]
    arrived = jnp.where(way == 1, near[None], jnp.where(way == 2, far[0][None], far[1][None]))
    row_ids = jnp.arange(kv_cache.shape[1], dtype=jnp.int32)
    arrived = jnp.where((row_ids[None, :] < arrival_len[:, None])[:, :, None, None], arrived, jnp.zeros((), jnp.bfloat16))
    rows = 16
    guests = jnp.pad(hidden[resident:].reshape(arrive * steps, width), ((0, rows - arrive * steps), (0, 0)))
    part_new, up_new = pl.pallas_call(
        functools.partial(arrive_kernel, spans, slots),
        out_shape=(shaped(arrive, rows, math.prod(unit_a[:2]), dtype=jnp.float32), shaped(arrive, *unit_b)),
        in_specs=[SMEM] * 3 + [VMEM] + [ANY] * 8,
        out_specs=(VMEM, VMEM),
        scratch_shapes=[pltpu.VMEM((arrive,) + unit_a, kind), pltpu.SemaphoreType.DMA((2 * arrive,))],
        cost_estimate=cost(arrive * (size_a + 2 * size_b), 2 * arrive * rows * size_a // 2),
    )(*plan, guests, z1, z2, z3, core_u, f0, f1, core_b, far_b)
    part_new = jnp.concatenate([part_new[a, a * steps : (a + 1) * steps] for a in range(arrive)], axis=0)
    shrink_new = total(part_new).reshape(arrive, steps, 2, -1)
    fresh_new = fresh_rows(base[resident:], shrink_new, up_new, arrival_len)
    move_out = attend(queries[resident:], arrived, arrival_len, fresh_new).astype(jnp.bfloat16)

    attn_out = jnp.concatenate([stay_out, move_out], axis=0)
    new_kv = jnp.concatenate([stay_kv, fresh_new], axis=0)
    installed_a, installed_b = pl.pallas_call(
        functools.partial(install_kernel, spans, slots),
        out_shape=(shaped(COPIES, *unit_a), shaped(COPIES, *unit_b)),
        in_specs=[SMEM] * 3 + [ANY] * 9,
        out_specs=(ANY, ANY),
        scratch_shapes=[
            pltpu.VMEM((COPIES,) + unit_a, kind),
            pltpu.VMEM((COPIES,) + unit_b, kind),
            pltpu.SemaphoreType.DMA((4 * COPIES,)),
        ],
        cost_estimate=cost(8 * size_a + 8 * size_b),
    )(*plan, z1, z2, z3, core_u, f0, f1, f2, core_b, far_b)
    return (attn_out, new_kv, arrived, installed_a, installed_b)


def solution(mesh):
    in_specs = (
        P(("parts", "replica"), None, "tensor"),
        P(("parts", "replica"), None, "tensor", None),
        P(("parts", "replica"), None, "tensor", None),
        P(None, "tensor", None),
        P(("parts", "replica"), None, None, "tensor"),
        P(("parts", "replica"), None, None, "tensor"),
        P("parts"),
        P("parts", None),
        P("parts", None),
        P("parts"),
        P("parts", None),
        P("parts"),
        P("parts", None),
    )
    out_specs = (
        P(("parts", "replica"), None, "tensor"),
        P(("parts", "replica"), None, "tensor", None),
        P(("parts", "replica"), None, "tensor", None),
        P(("parts", "replica"), None, None, "tensor"),
        P(("parts", "replica"), None, None, "tensor"),
    )
    local = paired if mesh.shape["replica"] == PAIRED and mesh.shape["tensor"] == TENSORS else general
    return jax.shard_map(local, mesh=mesh, in_specs=in_specs, out_specs=out_specs, check_vma=False)
```

```python
import functools
import math

import jax
import jax.numpy as jnp
from jax import lax
from jax.experimental import pallas as pl
from jax.experimental.pallas import tpu as pltpu
from jax.sharding import PartitionSpec as P

COPIES = 4


ADAPTER_SCALE = 2.0
ROPE_BASE = 500000.0


def rotate_keys(key_rows, positions):
    head_length = key_rows.shape[-1]
    half_size = head_length // 2
    frequency = ROPE_BASE ** (-(jnp.arange(half_size, dtype=jnp.float32) * 2.0 / head_length))
    angles = positions.astype(jnp.float32)[:, :, None, None] * frequency
    cosine = jnp.cos(angles)
    sine_val = jnp.sin(angles)
    first_half = key_rows[..., :half_size]
    second_half = key_rows[..., half_size:]
    return jnp.concatenate(
        [
            first_half * cosine - second_half * sine_val,
            second_half * cosine + first_half * sine_val,
        ],
        axis=-1,
    )


def attend(queries, stored, lengths_now, fresh_kv):
    request_slot_count, decode_step_count, heads_local, head_length = queries.shape
    local_key_value = stored.shape[2]
    group_size = heads_local // local_key_value
    grouped = queries.reshape(
        request_slot_count, decode_step_count, local_key_value, group_size, head_length
    )
    score_scale = 1.0 / math.sqrt(head_length)
    past_scores = (
        jnp.einsum(
            "msgjd,mcgd->msgjc",
            grouped,
            stored[..., :head_length],
            preferred_element_type=jnp.float32,
        )
        * score_scale
    )
    recent_scores = (
        jnp.einsum(
            "msgjd,mtgd->msgjt",
            grouped,
            fresh_kv[..., :head_length],
            preferred_element_type=jnp.float32,
        )
        * score_scale
    )
    row_ids = jnp.arange(stored.shape[1], dtype=jnp.int32)
    past_ok = (row_ids[None, :] < lengths_now[:, None])[:, None, None, None, :]
    step_ids = jnp.arange(decode_step_count, dtype=jnp.int32)
    recent_ok = (step_ids[None, :] <= step_ids[:, None])[None, :, None, None, :]
    past_scores = jnp.where(past_ok, past_scores, -jnp.inf)
    recent_scores = jnp.where(recent_ok, recent_scores, -jnp.inf)
    peak_score = jnp.maximum(jnp.max(past_scores, -1), jnp.max(recent_scores, -1))[..., None]
    past_exp = jnp.exp(past_scores - peak_score)
    recent_exp = jnp.exp(recent_scores - peak_score)
    denom_sum = jnp.sum(past_exp, -1, keepdims=True) + jnp.sum(recent_exp, -1, keepdims=True)
    past_w = (past_exp / denom_sum).astype(jnp.bfloat16)
    recent_w = (recent_exp / denom_sum).astype(jnp.bfloat16)
    mixed_out = jnp.einsum(
        "msgjc,mcgd->msgjd", past_w, stored[..., head_length:], preferred_element_type=jnp.float32
    )
    mixed_out = mixed_out + jnp.einsum(
        "msgjt,mtgd->msgjd",
        recent_w,
        fresh_kv[..., head_length:],
        preferred_element_type=jnp.float32,
    )
    return mixed_out.reshape(request_slot_count, decode_step_count, heads_local * head_length)


def general(
    hidden,
    queries,
    kv_cache,
    w_kv,
    store_a,
    store_b,
    lengths,
    arrival_from,
    arrival_slot,
    resident_adapter,
    arrival_adapter,
    hot_holder,
    hot_dest,
):
    my_index = lax.axis_index("replica")
    replicas = lax.axis_size("replica")
    resident = kv_cache.shape[0]
    arrive = arrival_from.shape[1]
    request_slot_count = resident + arrive
    decode_step_count = hidden.shape[1]
    head_length = queries.shape[3]
    local_key_value = kv_cache.shape[2]
    slot_total = store_a.shape[0]
    hot_total = hot_holder.shape[0]
    spans = hot_total // COPIES
    my_from = lax.dynamic_index_in_dim(arrival_from, my_index, 0, keepdims=False)
    my_slot = lax.dynamic_index_in_dim(arrival_slot, my_index, 0, keepdims=False)
    own_ids = my_index * resident + jnp.arange(resident, dtype=jnp.int32)
    leaving_ids = (arrival_from * resident + arrival_slot).reshape(-1)
    staying = jnp.logical_not(jnp.any(own_ids[:, None] == leaving_ids[None, :], axis=1))
    live_mask = jnp.concatenate([staying, jnp.ones((arrive,), bool)])
    own_len = lax.dynamic_slice_in_dim(lengths, my_index * resident, resident)
    arrival_len = jnp.take(lengths, my_from * resident + my_slot)
    seen_len = jnp.concatenate([own_len, arrival_len])
    takes_mine = arrival_from == my_index
    sends_any = jnp.any(takes_mine, axis=1)
    send_slot = jnp.sum(jnp.where(takes_mine, arrival_slot, 0), axis=1)
    outgoing = jnp.take(kv_cache, send_slot, axis=0)
    outgoing = jnp.where(sends_any[:, None, None, None], outgoing, jnp.zeros((), jnp.bfloat16))
    incoming = lax.all_to_all(outgoing, "replica", split_axis=0, concat_axis=0, tiled=True)
    blocks = hot_dest.reshape(COPIES, spans, hot_dest.shape[1])
    holder_grid = hot_holder.reshape(COPIES, spans)
    holder_rep = holder_grid // slot_total
    mine = holder_rep == my_index
    has_one = jnp.any(mine, axis=1)
    local_pick = jnp.sum(jnp.where(mine, holder_grid % slot_total, 0), axis=1)

    def spread_rows(store):
        rows = jnp.take(store, local_pick, axis=0)
        rows = jnp.where(has_one[:, None, None, None], rows, jnp.zeros((), jnp.bfloat16))
        return rows.reshape(COPIES, replicas, -1).transpose(1, 0, 2)

    got_a, got_b = (
        lax.all_to_all(spread_rows(store_a), "replica", split_axis=0, concat_axis=0, tiled=True),
        lax.all_to_all(spread_rows(store_b), "replica", split_axis=0, concat_axis=0, tiled=True),
    )
    replica_ids = jnp.arange(replicas, dtype=jnp.int32)
    member = jnp.any(blocks[:, :, :, None] == replica_ids[None, None, None, :], axis=2).astype(
        jnp.int32
    )
    source_rep = jnp.sum(member * holder_rep[:, :, None], axis=1)
    copy_ids = jnp.arange(COPIES, dtype=jnp.int32)
    route_a = got_a[source_rep.T, copy_ids[None, :]]
    route_b = got_b[source_rep.T, copy_ids[None, :]]
    recv_a, recv_b = (
        lax.all_to_all(route_a, "replica", split_axis=0, concat_axis=0, tiled=True),
        lax.all_to_all(route_b, "replica", split_axis=0, concat_axis=0, tiled=True),
    )
    installed_a = recv_a.transpose(1, 0, 2).reshape((COPIES,) + store_a.shape[1:])
    installed_b = recv_b.transpose(1, 0, 2).reshape((COPIES,) + store_b.shape[1:])
    own_adapter = lax.dynamic_slice_in_dim(resident_adapter, my_index * resident, resident)
    my_choice = lax.dynamic_index_in_dim(arrival_adapter, my_index, 0, keepdims=False)
    adapt_a = jnp.concatenate(
        [jnp.take(store_a, own_adapter, axis=0), jnp.take(installed_a, my_choice, axis=0)]
    )
    adapter_up_weight = jnp.concatenate(
        [jnp.take(store_b, own_adapter, axis=0), jnp.take(installed_b, my_choice, axis=0)]
    )
    partial_value = jnp.einsum(
        "msd,mpkd->mspk", hidden, adapt_a, preferred_element_type=jnp.float32
    )
    base_projection = jnp.einsum(
        "msd,dgc->msgc",
        lax.all_gather(hidden, "tensor", axis=2, tiled=True),
        w_kv,
        preferred_element_type=jnp.float32,
    )
    down_projected = lax.psum(partial_value, "tensor")
    down_projected = down_projected.astype(jnp.bfloat16)
    adapter_update = jnp.einsum(
        "gnot,gote->gnoe", down_projected, adapter_up_weight, preferred_element_type=jnp.float32
    )
    adapter_update = (
        adapter_update.reshape(
            request_slot_count, decode_step_count, 2, local_key_value, head_length
        )
        .transpose(0, 1, 3, 2, 4)
        .reshape(request_slot_count, decode_step_count, local_key_value, 2 * head_length)
    )
    unrotated_key_value = base_projection + ADAPTER_SCALE * adapter_update
    positions = seen_len[:, None] + jnp.arange(decode_step_count, dtype=jnp.int32)[None, :]
    fresh_kv = jnp.concatenate(
        [
            rotate_keys(unrotated_key_value[..., :head_length], positions),
            unrotated_key_value[..., head_length:],
        ],
        axis=-1,
    ).astype(jnp.bfloat16)
    stay_out = attend(queries[:resident], kv_cache, own_len, fresh_kv[:resident])
    arrived = jnp.take(incoming, my_from, axis=0)
    row_ids = jnp.arange(kv_cache.shape[1], dtype=jnp.int32)
    arrived = jnp.where(
        (row_ids[None, :] < arrival_len[:, None])[:, :, None, None],
        arrived,
        jnp.zeros((), jnp.bfloat16),
    )
    move_out = attend(queries[resident:], arrived, arrival_len, fresh_kv[resident:])
    mixed_out = jnp.concatenate([stay_out, move_out], axis=0)
    attn_out = jnp.where(live_mask[:, None, None], mixed_out, 0.0).astype(jnp.bfloat16)
    new_kv = jnp.where(live_mask[:, None, None, None], fresh_kv, jnp.zeros((), jnp.bfloat16))
    return (attn_out, new_kv, arrived, installed_a, installed_b)


PAIRED = 4
TENSORS = 4


def needed_first(adapter_ref, dest):
    first, second = adapter_ref[0, dest], adapter_ref[1, dest]
    ids = range(1, COPIES)
    keys = [jnp.where(first == c, 0, jnp.where(second == c, 1, 2 + c)) for c in ids]
    place = [sum(jnp.where(other < key, 1, 0) for other in keys) for key in keys]
    order = [sum(jnp.where(place[c - 1] == j, c, 0) for c in ids) for j in range(COPIES - 1)]
    return order, place


def held_slot(holder_ref, spans, slots, replica, copy_id):
    found = jnp.int32(0)
    for s in range(spans):
        holder = holder_ref[copy_id * spans + s]
        found = jnp.where(holder // slots == replica, holder % slots, found)
    return found


def holder_of(holder_ref, dest_ref, spans, dest, copy_id):
    found = jnp.int32(0)
    for s in range(spans):
        row = copy_id * spans + s
        found = jnp.where(dest_ref[0, row] == dest, holder_ref[row], found)
    return found


class Staged:
    def __init__(self, sems):
        self.sems, self.jobs = sems, []

    def go(self, options, stage, dst):
        sem = self.sems.at[len(self.jobs)]
        for condition, src in options:
            if condition is None:
                pltpu.make_async_copy(src, stage, sem).start()
            else:

                @pl.when(condition)
                def _():
                    pltpu.make_async_copy(src, stage, sem).start()

        self.jobs.append((stage, dst))

    def arrived(self, i):
        stage, _ = self.jobs[i]
        pltpu.make_async_copy(stage, stage, self.sems.at[i]).wait()

    def finish(self):
        half = len(self.jobs)
        for i, (stage, dst) in enumerate(self.jobs):
            self.arrived(i)
            pltpu.make_async_copy(stage, dst, self.sems.at[half + i]).start()
        for i, (stage, dst) in enumerate(self.jobs):
            pltpu.make_async_copy(stage, dst, self.sems.at[half + i]).wait()


def pack_kernel(spans, slots, from_hbm, slot_hbm, adapter_hbm, holder_hbm, a_ref, b_ref, kv_ref,
                z_out, u_out, b_out, k1_out, k2_out, k3_out,
                from_ref, slot_ref, adapter_ref, holder_ref, a_stage, b_stage, k_stage, small_sems, sems):
    me = lax.axis_index("replica")
    small = [
        pltpu.make_async_copy(src, dst, small_sems.at[i])
        for i, (src, dst) in enumerate(
            ((adapter_hbm, adapter_ref), (holder_hbm, holder_ref), (from_hbm, from_ref), (slot_hbm, slot_ref))
        )
    ]
    for copy in small:
        copy.start()
    for copy in small:
        copy.wait()
    staged = Staged(sems)
    order, _ = needed_first(adapter_ref, me ^ 3)
    outs = [z_out] + [u_out.at[j] for j in range(COPIES - 1)]
    for j, c in enumerate([0] + order):
        staged.go([(None, a_ref.at[held_slot(holder_ref, spans, slots, me, c)])], a_stage.at[j], outs[j])
        if j == 0:
            for c in range(COPIES):
                staged.go([(None, b_ref.at[held_slot(holder_ref, spans, slots, me, c)])], b_stage.at[c], b_out.at[c])
            for k, out in ((1, k1_out), (2, k2_out), (3, k3_out)):
                chosen = jnp.int32(0)
                for a in range(2):
                    chosen = jnp.where(from_ref[a, me ^ k] == me, slot_ref[a, me ^ k], chosen)
                staged.go([(None, kv_ref.at[chosen])], k_stage.at[k - 1], out)
    staged.finish()


def pick_kernel(spans, slots, places, copies, adapter_ref, holder_ref, dest_ref, a_ref, b_ref, core_a, core_b, *rest):
    outs, (a_stage, b_stage, sems) = rest[:-3], rest[-3:]
    me = lax.axis_index("replica")
    order, _ = needed_first(adapter_ref, me ^ 2)
    staged = Staged(sems)

    def options(c, store, core):
        holder = holder_of(holder_ref, dest_ref, spans, me ^ 2, c)
        mine = holder // slots == me
        return [(mine, store.at[holder % slots]), (jnp.logical_not(mine), core)]

    for i, j in enumerate(places):
        staged.go(options(order[j], a_ref, core_a.at[j]), a_stage.at[i], outs[i])
    for c in range(copies):
        staged.go(options(c, b_ref, core_b.at[c]), b_stage.at[c], outs[-1].at[c])
    staged.finish()


def sources(spans, slots, adapter_ref, holder_ref, dest_ref, z_refs, near_refs, far_refs, near_b, far_b):
    me = lax.axis_index("replica")
    _, place_far = needed_first(adapter_ref, me)
    _, place_near = needed_first(adapter_ref, me ^ 2)

    def at(places, c):
        return sum(jnp.where(c == i + 1, place, 0) for i, place in enumerate(places))

    def options(c):
        holder = holder_of(holder_ref, dest_ref, spans, me, c) // slots
        near = holder == (me ^ 1)
        far = jnp.logical_not(near)
        of_a = []
        zero = c == 0
        for k, ref in enumerate(z_refs):
            of_a.append((jnp.logical_and(zero, holder == (me ^ (k + 1))), ref))
        for side, places, refs in ((near, place_near, near_refs), (far, place_far, far_refs)):
            for j, ref in enumerate(refs):
                here = jnp.logical_and(side, at(places, c) == j)
                of_a.append((jnp.logical_and(c != 0, here), ref))
        return of_a, [(near, near_b.at[c]), (far, far_b.at[c])]

    return options


def arrive_kernel(spans, slots, adapter_ref, holder_ref, dest_ref, hid_ref, z1, z2, z3, u, f0, f1, cb, xb,
                  out_ref, b_out, units, sems):
    me = lax.axis_index("replica")
    options = sources(
        spans, slots, adapter_ref, holder_ref, dest_ref, (z1, z2, z3), [u.at[j] for j in range(COPIES - 1)], (f0, f1), cb, xb
    )
    staged = Staged(sems)
    for a in range(2):
        of_a, of_b = options(adapter_ref[a, me])
        staged.go(of_a, units.at[a], None)
        staged.go(of_b, b_out.at[a], None)
    for a in range(2):
        staged.arrived(2 * a)
        unit = units[a].reshape(units.shape[1] * units.shape[2], units.shape[3])
        out_ref[a] = lax.dot_general(hid_ref[...], unit, (((1,), (1,)), ((), ())), preferred_element_type=jnp.float32)
        staged.arrived(2 * a + 1)


def install_kernel(spans, slots, adapter_ref, holder_ref, dest_ref, z1, z2, z3, u, f0, f1, f2, cb, xb,
                   a_out, b_out, a_stage, b_stage, sems):
    options = sources(
        spans, slots, adapter_ref, holder_ref, dest_ref, (z1, z2, z3), [u.at[j] for j in range(COPIES - 1)], (f0, f1, f2), cb, xb
    )
    staged = Staged(sems)
    for c in range(COPIES):
        of_a, of_b = options(jnp.int32(c))
        staged.go(of_a, a_stage.at[c], a_out.at[c])
        staged.go(of_b, b_stage.at[c], b_out.at[c])
    staged.finish()


SMEM = pl.BlockSpec(memory_space=pltpu.SMEM)
ANY = pl.BlockSpec(memory_space=pl.ANY)
VMEM = pl.BlockSpec(memory_space=pltpu.VMEM)


def paired(
    hidden,
    queries,
    kv_cache,
    w_kv,
    store_a,
    store_b,
    lengths,
    arrival_from,
    arrival_slot,
    resident_adapter,
    arrival_adapter,
    hot_holder,
    hot_dest,
):
    me = lax.axis_index("replica")
    tensor_index = lax.axis_index("tensor")
    resident, arrive = kv_cache.shape[0], arrival_from.shape[1]
    requests, steps, width = hidden.shape
    head_length, heads = queries.shape[3], kv_cache.shape[2]
    slots = store_a.shape[0]
    spans = hot_holder.shape[0] // COPIES
    kind = store_a.dtype
    unit_a, unit_b, unit_k = store_a.shape[1:], store_b.shape[1:], kv_cache.shape[1:]

    def shaped(*shape, dtype=kind):
        return jax.ShapeDtypeStruct(shape, dtype)

    def swap(array, k):
        return lax.ppermute(array, "replica", [(i, i ^ k) for i in range(PAIRED)])

    def mirror(array, k):
        return lax.ppermute(array, "tensor", [(i, i ^ k) for i in range(TENSORS)])

    def cost(bytes_accessed, flops=0):
        return pl.CostEstimate(flops=flops, bytes_accessed=bytes_accessed, transcendentals=0)

    size_a, size_b = 2 * math.prod(unit_a), 2 * math.prod(unit_b)

    plan = (arrival_adapter.T, hot_holder, hot_dest.T)
    leave = (arrival_from.T, arrival_slot.T)

    z, u, b_all, k1, k2, k3 = pl.pallas_call(
        functools.partial(pack_kernel, spans, slots),
        out_shape=(
            shaped(*unit_a), shaped(COPIES - 1, *unit_a), shaped(COPIES, *unit_b),
            shaped(*unit_k), shaped(*unit_k), shaped(*unit_k),
        ),
        in_specs=[ANY] * 7,
        out_specs=(ANY,) * 6,
        scratch_shapes=[pltpu.SMEM(x.shape, x.dtype) for x in leave + plan[:2]]
        + [
            pltpu.VMEM((COPIES,) + unit_a, kind),
            pltpu.VMEM((COPIES,) + unit_b, kind),
            pltpu.VMEM((3,) + unit_k, kind),
            pltpu.SemaphoreType.DMA((4,)),
            pltpu.SemaphoreType.DMA((2 * (2 * COPIES + 3),)),
        ],
        cost_estimate=cost(8 * size_a + 8 * size_b),
    )(*leave, *plan[:2], store_a, store_b, kv_cache)
    z2 = swap(z, 2)
    core_u, core_b = swap(u, 1), swap(b_all, 1)
    far = (swap(k2, 2), swap(k3, 3))

    u, hidden = lax.optimization_barrier((u, hidden))
    own_adapter = lax.dynamic_slice_in_dim(resident_adapter, me * resident, resident)
    every = jnp.einsum("msd,epkd->msepk", hidden[:resident], store_a, preferred_element_type=jnp.float32)
    is_own = own_adapter[:, None] == jnp.arange(slots, dtype=jnp.int32)[None, :]
    part_own = jnp.sum(jnp.where(is_own[:, None, :, None, None], every, 0.0), axis=2)
    part_own, core_u = lax.optimization_barrier((part_own, core_u))
    _, sent = lax.optimization_barrier((core_b, hidden))
    other = mirror(sent, 2)

    def pick(places, copies, core):
        out = pl.pallas_call(
            functools.partial(pick_kernel, spans, slots, places, copies),
            out_shape=tuple(shaped(*unit_a) for _ in places) + (shaped(COPIES, *unit_b),) * (copies > 0),
            in_specs=[SMEM] * 3 + [ANY] * 4,
            out_specs=(ANY,) * (len(places) + (copies > 0)),
            scratch_shapes=[
                pltpu.VMEM((len(places),) + unit_a, kind),
                pltpu.VMEM((COPIES,) + unit_b, kind),
                pltpu.SemaphoreType.DMA((2 * (len(places) + copies),)),
            ],
            cost_estimate=cost(2 * len(places) * size_a + 2 * copies * size_b),
        )(*plan, store_a, store_b, core, core_b)
        return out

    to0, to1, to2, to_b = pick((0, 1, 2), COPIES, core_u)
    f0 = swap(to0, 2)

    z2, far, to1, to_b = lax.optimization_barrier((z2, far, to1, to_b))
    f1, far_b = swap(to1, 2), swap(to_b, 2)

    _, other, lengths, queries, k1 = lax.optimization_barrier((to0, other, lengths, queries, k1))
    near = swap(k1, 1)

    def total(part):
        out = part
        for k in (2, 1):
            out = out + mirror(out, k)
        return out.astype(jnp.bfloat16)

    high, low = tensor_index >= 2, tensor_index % 2 == 1
    halves = jnp.concatenate([jnp.where(high, other, sent), jnp.where(high, sent, other)], axis=2)
    other = mirror(halves, 1)
    even, odd = jnp.where(low, other, halves), jnp.where(low, halves, other)
    whole = jnp.concatenate([even[..., :width], odd[..., :width], even[..., width:], odd[..., width:]], axis=2)
    base = jnp.einsum("msd,dgc->msgc", whole, w_kv, preferred_element_type=jnp.float32)
    f0, base, to2, z, z2 = lax.optimization_barrier((f0, base, to2, z, z2))
    f2 = swap(to2, 2)
    z1, z3 = swap(z, 1), swap(z2, 1)

    my_from = lax.dynamic_index_in_dim(arrival_from, me, 0, keepdims=False)
    my_slot = lax.dynamic_index_in_dim(arrival_slot, me, 0, keepdims=False)
    own_ids = me * resident + jnp.arange(resident, dtype=jnp.int32)
    leaving = (arrival_from * resident + arrival_slot).reshape(-1)
    staying = jnp.logical_not(jnp.any(own_ids[:, None] == leaving[None, :], axis=1))
    own_len = lax.dynamic_slice_in_dim(lengths, me * resident, resident)
    arrival_len = jnp.take(lengths, my_from * resident + my_slot)

    def fresh_rows(base_rows, shrink, up, seen):
        count = base_rows.shape[0]
        update = jnp.einsum("gnot,gote->gnoe", shrink, up, preferred_element_type=jnp.float32)
        update = update.reshape(count, steps, 2, heads, head_length).transpose(0, 1, 3, 2, 4)
        raw = base_rows + ADAPTER_SCALE * update.reshape(count, steps, heads, 2 * head_length)
        positions = seen[:, None] + jnp.arange(steps, dtype=jnp.int32)[None, :]
        turned = rotate_keys(raw[..., :head_length], positions)
        return jnp.concatenate([turned, raw[..., head_length:]], axis=-1).astype(jnp.bfloat16)

    up_own = jnp.take(store_b, own_adapter, axis=0)

    way = (my_from ^ me)[:, None, None, None]
    arrived = jnp.where(way == 1, near[None], jnp.where(way == 2, far[0][None], far[1][None]))
    row_ids = jnp.arange(kv_cache.shape[1], dtype=jnp.int32)
    arrived = jnp.where((row_ids[None, :] < arrival_len[:, None])[:, :, None, None], arrived, jnp.zeros((), jnp.bfloat16))
    rows = 16
    guests = jnp.pad(hidden[resident:].reshape(arrive * steps, width), ((0, rows - arrive * steps), (0, 0)))
    part_new, up_new = pl.pallas_call(
        functools.partial(arrive_kernel, spans, slots),
        out_shape=(shaped(arrive, rows, math.prod(unit_a[:2]), dtype=jnp.float32), shaped(arrive, *unit_b)),
        in_specs=[SMEM] * 3 + [VMEM] + [ANY] * 8,
        out_specs=(VMEM, VMEM),
        scratch_shapes=[pltpu.VMEM((arrive,) + unit_a, kind), pltpu.SemaphoreType.DMA((2 * arrive,))],
        cost_estimate=cost(arrive * (size_a + 2 * size_b), 2 * arrive * rows * size_a // 2),
    )(*plan, guests, z1, z2, z3, core_u, f0, f1, core_b, far_b)
    part = jnp.concatenate(
        [part_own.reshape(resident * steps, -1)]
        + [part_new[a, a * steps : (a + 1) * steps] for a in range(arrive)],
        axis=0,
    )
    shrink = total(part).reshape(requests, steps, 2, -1)

    seen = jnp.concatenate([own_len, arrival_len])
    live = jnp.concatenate([staying, jnp.ones((arrive,), bool)])
    fresh = fresh_rows(base, shrink, jnp.concatenate([up_own, up_new]), seen)
    mixed = attend(queries, jnp.concatenate([kv_cache, arrived]), seen, fresh)
    attn_out = jnp.where(live[:, None, None], mixed, 0.0).astype(jnp.bfloat16)
    new_kv = jnp.where(live[:, None, None, None], fresh, jnp.zeros((), jnp.bfloat16))
    installed_a, installed_b = pl.pallas_call(
        functools.partial(install_kernel, spans, slots),
        out_shape=(shaped(COPIES, *unit_a), shaped(COPIES, *unit_b)),
        in_specs=[SMEM] * 3 + [ANY] * 9,
        out_specs=(ANY, ANY),
        scratch_shapes=[
            pltpu.VMEM((COPIES,) + unit_a, kind),
            pltpu.VMEM((COPIES,) + unit_b, kind),
            pltpu.SemaphoreType.DMA((4 * COPIES,)),
        ],
        cost_estimate=cost(8 * size_a + 8 * size_b),
    )(*plan, z1, z2, z3, core_u, f0, f1, f2, core_b, far_b)
    return (attn_out, new_kv, arrived, installed_a, installed_b)


def solution(mesh):
    in_specs = (
        P(("parts", "replica"), None, "tensor"),
        P(("parts", "replica"), None, "tensor", None),
        P(("parts", "replica"), None, "tensor", None),
        P(None, "tensor", None),
        P(("parts", "replica"), None, None, "tensor"),
        P(("parts", "replica"), None, None, "tensor"),
        P("parts"),
        P("parts", None),
        P("parts", None),
        P("parts"),
        P("parts", None),
        P("parts"),
        P("parts", None),
    )
    out_specs = (
        P(("parts", "replica"), None, "tensor"),
        P(("parts", "replica"), None, "tensor", None),
        P(("parts", "replica"), None, "tensor", None),
        P(("parts", "replica"), None, None, "tensor"),
        P(("parts", "replica"), None, None, "tensor"),
    )
    local = paired if mesh.shape["replica"] == PAIRED and mesh.shape["tensor"] == TENSORS else general
    return jax.shard_map(local, mesh=mesh, in_specs=in_specs, out_specs=out_specs, check_vma=False)
```

```python
import functools
import math

import jax
import jax.numpy as jnp
from jax import lax
from jax.experimental import pallas as pl
from jax.experimental.pallas import tpu as pltpu
from jax.sharding import PartitionSpec as P

COPIES = 4


ADAPTER_SCALE = 2.0
ROPE_BASE = 500000.0


def rotate_keys(key_rows, positions):
    head_length = key_rows.shape[-1]
    half_size = head_length // 2
    frequency = ROPE_BASE ** (-(jnp.arange(half_size, dtype=jnp.float32) * 2.0 / head_length))
    angles = positions.astype(jnp.float32)[:, :, None, None] * frequency
    cosine = jnp.cos(angles)
    sine_val = jnp.sin(angles)
    first_half = key_rows[..., :half_size]
    second_half = key_rows[..., half_size:]
    return jnp.concatenate(
        [
            first_half * cosine - second_half * sine_val,
            second_half * cosine + first_half * sine_val,
        ],
        axis=-1,
    )


def attend(queries, stored, lengths_now, fresh_kv):
    request_slot_count, decode_step_count, heads_local, head_length = queries.shape
    local_key_value = stored.shape[2]
    group_size = heads_local // local_key_value
    grouped = queries.reshape(
        request_slot_count, decode_step_count, local_key_value, group_size, head_length
    )
    score_scale = 1.0 / math.sqrt(head_length)
    past_scores = (
        jnp.einsum(
            "msgjd,mcgd->msgjc",
            grouped,
            stored[..., :head_length],
            preferred_element_type=jnp.float32,
        )
        * score_scale
    )
    recent_scores = (
        jnp.einsum(
            "msgjd,mtgd->msgjt",
            grouped,
            fresh_kv[..., :head_length],
            preferred_element_type=jnp.float32,
        )
        * score_scale
    )
    row_ids = jnp.arange(stored.shape[1], dtype=jnp.int32)
    past_ok = (row_ids[None, :] < lengths_now[:, None])[:, None, None, None, :]
    step_ids = jnp.arange(decode_step_count, dtype=jnp.int32)
    recent_ok = (step_ids[None, :] <= step_ids[:, None])[None, :, None, None, :]
    past_scores = jnp.where(past_ok, past_scores, -jnp.inf)
    recent_scores = jnp.where(recent_ok, recent_scores, -jnp.inf)
    peak_score = jnp.maximum(jnp.max(past_scores, -1), jnp.max(recent_scores, -1))[..., None]
    past_exp = jnp.exp(past_scores - peak_score)
    recent_exp = jnp.exp(recent_scores - peak_score)
    denom_sum = jnp.sum(past_exp, -1, keepdims=True) + jnp.sum(recent_exp, -1, keepdims=True)
    past_w = (past_exp / denom_sum).astype(jnp.bfloat16)
    recent_w = (recent_exp / denom_sum).astype(jnp.bfloat16)
    mixed_out = jnp.einsum(
        "msgjc,mcgd->msgjd", past_w, stored[..., head_length:], preferred_element_type=jnp.float32
    )
    mixed_out = mixed_out + jnp.einsum(
        "msgjt,mtgd->msgjd",
        recent_w,
        fresh_kv[..., head_length:],
        preferred_element_type=jnp.float32,
    )
    return mixed_out.reshape(request_slot_count, decode_step_count, heads_local * head_length)


def general(
    hidden,
    queries,
    kv_cache,
    w_kv,
    store_a,
    store_b,
    lengths,
    arrival_from,
    arrival_slot,
    resident_adapter,
    arrival_adapter,
    hot_holder,
    hot_dest,
):
    my_index = lax.axis_index("replica")
    replicas = lax.axis_size("replica")
    resident = kv_cache.shape[0]
    arrive = arrival_from.shape[1]
    request_slot_count = resident + arrive
    decode_step_count = hidden.shape[1]
    head_length = queries.shape[3]
    local_key_value = kv_cache.shape[2]
    slot_total = store_a.shape[0]
    hot_total = hot_holder.shape[0]
    spans = hot_total // COPIES
    my_from = lax.dynamic_index_in_dim(arrival_from, my_index, 0, keepdims=False)
    my_slot = lax.dynamic_index_in_dim(arrival_slot, my_index, 0, keepdims=False)
    own_ids = my_index * resident + jnp.arange(resident, dtype=jnp.int32)
    leaving_ids = (arrival_from * resident + arrival_slot).reshape(-1)
    staying = jnp.logical_not(jnp.any(own_ids[:, None] == leaving_ids[None, :], axis=1))
    live_mask = jnp.concatenate([staying, jnp.ones((arrive,), bool)])
    own_len = lax.dynamic_slice_in_dim(lengths, my_index * resident, resident)
    arrival_len = jnp.take(lengths, my_from * resident + my_slot)
    seen_len = jnp.concatenate([own_len, arrival_len])
    takes_mine = arrival_from == my_index
    sends_any = jnp.any(takes_mine, axis=1)
    send_slot = jnp.sum(jnp.where(takes_mine, arrival_slot, 0), axis=1)
    outgoing = jnp.take(kv_cache, send_slot, axis=0)
    outgoing = jnp.where(sends_any[:, None, None, None], outgoing, jnp.zeros((), jnp.bfloat16))
    incoming = lax.all_to_all(outgoing, "replica", split_axis=0, concat_axis=0, tiled=True)
    blocks = hot_dest.reshape(COPIES, spans, hot_dest.shape[1])
    holder_grid = hot_holder.reshape(COPIES, spans)
    holder_rep = holder_grid // slot_total
    mine = holder_rep == my_index
    has_one = jnp.any(mine, axis=1)
    local_pick = jnp.sum(jnp.where(mine, holder_grid % slot_total, 0), axis=1)

    def spread_rows(store):
        rows = jnp.take(store, local_pick, axis=0)
        rows = jnp.where(has_one[:, None, None, None], rows, jnp.zeros((), jnp.bfloat16))
        return rows.reshape(COPIES, replicas, -1).transpose(1, 0, 2)

    got_a, got_b = (
        lax.all_to_all(spread_rows(store_a), "replica", split_axis=0, concat_axis=0, tiled=True),
        lax.all_to_all(spread_rows(store_b), "replica", split_axis=0, concat_axis=0, tiled=True),
    )
    replica_ids = jnp.arange(replicas, dtype=jnp.int32)
    member = jnp.any(blocks[:, :, :, None] == replica_ids[None, None, None, :], axis=2).astype(
        jnp.int32
    )
    source_rep = jnp.sum(member * holder_rep[:, :, None], axis=1)
    copy_ids = jnp.arange(COPIES, dtype=jnp.int32)
    route_a = got_a[source_rep.T, copy_ids[None, :]]
    route_b = got_b[source_rep.T, copy_ids[None, :]]
    recv_a, recv_b = (
        lax.all_to_all(route_a, "replica", split_axis=0, concat_axis=0, tiled=True),
        lax.all_to_all(route_b, "replica", split_axis=0, concat_axis=0, tiled=True),
    )
    installed_a = recv_a.transpose(1, 0, 2).reshape((COPIES,) + store_a.shape[1:])
    installed_b = recv_b.transpose(1, 0, 2).reshape((COPIES,) + store_b.shape[1:])
    own_adapter = lax.dynamic_slice_in_dim(resident_adapter, my_index * resident, resident)
    my_choice = lax.dynamic_index_in_dim(arrival_adapter, my_index, 0, keepdims=False)
    adapt_a = jnp.concatenate(
        [jnp.take(store_a, own_adapter, axis=0), jnp.take(installed_a, my_choice, axis=0)]
    )
    adapter_up_weight = jnp.concatenate(
        [jnp.take(store_b, own_adapter, axis=0), jnp.take(installed_b, my_choice, axis=0)]
    )
    partial_value = jnp.einsum(
        "msd,mpkd->mspk", hidden, adapt_a, preferred_element_type=jnp.float32
    )
    base_projection = jnp.einsum(
        "msd,dgc->msgc",
        lax.all_gather(hidden, "tensor", axis=2, tiled=True),
        w_kv,
        preferred_element_type=jnp.float32,
    )
    down_projected = lax.psum(partial_value, "tensor")
    down_projected = down_projected.astype(jnp.bfloat16)
    adapter_update = jnp.einsum(
        "gnot,gote->gnoe", down_projected, adapter_up_weight, preferred_element_type=jnp.float32
    )
    adapter_update = (
        adapter_update.reshape(
            request_slot_count, decode_step_count, 2, local_key_value, head_length
        )
        .transpose(0, 1, 3, 2, 4)
        .reshape(request_slot_count, decode_step_count, local_key_value, 2 * head_length)
    )
    unrotated_key_value = base_projection + ADAPTER_SCALE * adapter_update
    positions = seen_len[:, None] + jnp.arange(decode_step_count, dtype=jnp.int32)[None, :]
    fresh_kv = jnp.concatenate(
        [
            rotate_keys(unrotated_key_value[..., :head_length], positions),
            unrotated_key_value[..., head_length:],
        ],
        axis=-1,
    ).astype(jnp.bfloat16)
    stay_out = attend(queries[:resident], kv_cache, own_len, fresh_kv[:resident])
    arrived = jnp.take(incoming, my_from, axis=0)
    row_ids = jnp.arange(kv_cache.shape[1], dtype=jnp.int32)
    arrived = jnp.where(
        (row_ids[None, :] < arrival_len[:, None])[:, :, None, None],
        arrived,
        jnp.zeros((), jnp.bfloat16),
    )
    move_out = attend(queries[resident:], arrived, arrival_len, fresh_kv[resident:])
    mixed_out = jnp.concatenate([stay_out, move_out], axis=0)
    attn_out = jnp.where(live_mask[:, None, None], mixed_out, 0.0).astype(jnp.bfloat16)
    new_kv = jnp.where(live_mask[:, None, None, None], fresh_kv, jnp.zeros((), jnp.bfloat16))
    return (attn_out, new_kv, arrived, installed_a, installed_b)


PAIRED = 4
TENSORS = 4


def needed_first(adapter_ref, dest):
    first, second = adapter_ref[0, dest], adapter_ref[1, dest]
    ids = range(1, COPIES)
    keys = [jnp.where(first == c, 0, jnp.where(second == c, 1, 2 + c)) for c in ids]
    place = [sum(jnp.where(other < key, 1, 0) for other in keys) for key in keys]
    order = [sum(jnp.where(place[c - 1] == j, c, 0) for c in ids) for j in range(COPIES - 1)]
    return order, place


def held_slot(holder_ref, spans, slots, replica, copy_id):
    found = jnp.int32(0)
    for s in range(spans):
        holder = holder_ref[copy_id * spans + s]
        found = jnp.where(holder // slots == replica, holder % slots, found)
    return found


def holder_of(holder_ref, dest_ref, spans, dest, copy_id):
    found = jnp.int32(0)
    for s in range(spans):
        row = copy_id * spans + s
        found = jnp.where(dest_ref[0, row] == dest, holder_ref[row], found)
    return found


class Staged:
    def __init__(self, sems):
        self.sems, self.jobs = sems, []

    def go(self, options, stage, dst):
        sem = self.sems.at[len(self.jobs)]
        for condition, src in options:
            if condition is None:
                pltpu.make_async_copy(src, stage, sem).start()
            else:

                @pl.when(condition)
                def _():
                    pltpu.make_async_copy(src, stage, sem).start()

        self.jobs.append((stage, dst))

    def arrived(self, i):
        stage, _ = self.jobs[i]
        pltpu.make_async_copy(stage, stage, self.sems.at[i]).wait()

    def finish(self):
        half = len(self.jobs)
        for i, (stage, dst) in enumerate(self.jobs):
            self.arrived(i)
            pltpu.make_async_copy(stage, dst, self.sems.at[half + i]).start()
        for i, (stage, dst) in enumerate(self.jobs):
            pltpu.make_async_copy(stage, dst, self.sems.at[half + i]).wait()


def pack_kernel(spans, slots, from_hbm, slot_hbm, adapter_hbm, holder_hbm, a_ref, b_ref, kv_ref,
                z_out, u_out, b_out, k1_out, k2_out, k3_out,
                from_ref, slot_ref, adapter_ref, holder_ref, a_stage, b_stage, k_stage, small_sems, sems):
    me = lax.axis_index("replica")
    small = [
        pltpu.make_async_copy(src, dst, small_sems.at[i])
        for i, (src, dst) in enumerate(
            ((adapter_hbm, adapter_ref), (holder_hbm, holder_ref), (from_hbm, from_ref), (slot_hbm, slot_ref))
        )
    ]
    for copy in small:
        copy.start()
    for copy in small:
        copy.wait()
    staged = Staged(sems)
    order, _ = needed_first(adapter_ref, me ^ 3)
    outs = [z_out] + [u_out.at[j] for j in range(COPIES - 1)]
    for j, c in enumerate([0] + order):
        staged.go([(None, a_ref.at[held_slot(holder_ref, spans, slots, me, c)])], a_stage.at[j], outs[j])
        if j == 0:
            for c in range(COPIES):
                staged.go([(None, b_ref.at[held_slot(holder_ref, spans, slots, me, c)])], b_stage.at[c], b_out.at[c])
            for k, out in ((1, k1_out), (2, k2_out), (3, k3_out)):
                chosen = jnp.int32(0)
                for a in range(2):
                    chosen = jnp.where(from_ref[a, me ^ k] == me, slot_ref[a, me ^ k], chosen)
                staged.go([(None, kv_ref.at[chosen])], k_stage.at[k - 1], out)
    staged.finish()


def pick_kernel(spans, slots, places, copies, adapter_ref, holder_ref, dest_ref, a_ref, b_ref, core_a, core_b, *rest):
    outs, (a_stage, b_stage, sems) = rest[:-3], rest[-3:]
    me = lax.axis_index("replica")
    order, _ = needed_first(adapter_ref, me ^ 2)
    staged = Staged(sems)

    def options(c, store, core):
        holder = holder_of(holder_ref, dest_ref, spans, me ^ 2, c)
        mine = holder // slots == me
        return [(mine, store.at[holder % slots]), (jnp.logical_not(mine), core)]

    for i, j in enumerate(places):
        staged.go(options(order[j], a_ref, core_a.at[j]), a_stage.at[i], outs[i])
    for c in range(copies):
        staged.go(options(c, b_ref, core_b.at[c]), b_stage.at[c], outs[-1].at[c])
    staged.finish()


def sources(spans, slots, adapter_ref, holder_ref, dest_ref, z_refs, near_refs, far_refs, near_b, far_b):
    me = lax.axis_index("replica")
    _, place_far = needed_first(adapter_ref, me)
    _, place_near = needed_first(adapter_ref, me ^ 2)

    def at(places, c):
        return sum(jnp.where(c == i + 1, place, 0) for i, place in enumerate(places))

    def options(c):
        holder = holder_of(holder_ref, dest_ref, spans, me, c) // slots
        near = holder == (me ^ 1)
        far = jnp.logical_not(near)
        of_a = []
        zero = c == 0
        for k, ref in enumerate(z_refs):
            of_a.append((jnp.logical_and(zero, holder == (me ^ (k + 1))), ref))
        for side, places, refs in ((near, place_near, near_refs), (far, place_far, far_refs)):
            for j, ref in enumerate(refs):
                here = jnp.logical_and(side, at(places, c) == j)
                of_a.append((jnp.logical_and(c != 0, here), ref))
        return of_a, [(near, near_b.at[c]), (far, far_b.at[c])]

    return options


def arrive_kernel(spans, slots, adapter_ref, holder_ref, dest_ref, hid_ref, z1, z2, z3, u, f0, f1, cb, xb,
                  out_ref, b_out, units, sems):
    me = lax.axis_index("replica")
    options = sources(
        spans, slots, adapter_ref, holder_ref, dest_ref, (z1, z2, z3), [u.at[j] for j in range(COPIES - 1)], (f0, f1), cb, xb
    )
    staged = Staged(sems)
    for a in range(2):
        of_a, of_b = options(adapter_ref[a, me])
        staged.go(of_a, units.at[a], None)
        staged.go(of_b, b_out.at[a], None)
    for a in range(2):
        staged.arrived(2 * a)
        unit = units[a].reshape(units.shape[1] * units.shape[2], units.shape[3])
        out_ref[a] = lax.dot_general(hid_ref[...], unit, (((1,), (1,)), ((), ())), preferred_element_type=jnp.float32)
        staged.arrived(2 * a + 1)


def install_kernel(spans, slots, adapter_ref, holder_ref, dest_ref, z1, z2, z3, u, f0, f1, f2, cb, xb,
                   a_out, b_out, a_stage, b_stage, sems):
    options = sources(
        spans, slots, adapter_ref, holder_ref, dest_ref, (z1, z2, z3), [u.at[j] for j in range(COPIES - 1)], (f0, f1, f2), cb, xb
    )
    staged = Staged(sems)
    for c in range(COPIES):
        of_a, of_b = options(jnp.int32(c))
        staged.go(of_a, a_stage.at[c], a_out.at[c])
        staged.go(of_b, b_stage.at[c], b_out.at[c])
    staged.finish()


SMEM = pl.BlockSpec(memory_space=pltpu.SMEM)
ANY = pl.BlockSpec(memory_space=pl.ANY)
VMEM = pl.BlockSpec(memory_space=pltpu.VMEM)


def paired(
    hidden,
    queries,
    kv_cache,
    w_kv,
    store_a,
    store_b,
    lengths,
    arrival_from,
    arrival_slot,
    resident_adapter,
    arrival_adapter,
    hot_holder,
    hot_dest,
):
    me = lax.axis_index("replica")
    tensor_index = lax.axis_index("tensor")
    resident, arrive = kv_cache.shape[0], arrival_from.shape[1]
    requests, steps, width = hidden.shape
    head_length, heads = queries.shape[3], kv_cache.shape[2]
    slots = store_a.shape[0]
    spans = hot_holder.shape[0] // COPIES
    kind = store_a.dtype
    unit_a, unit_b, unit_k = store_a.shape[1:], store_b.shape[1:], kv_cache.shape[1:]

    def shaped(*shape, dtype=kind):
        return jax.ShapeDtypeStruct(shape, dtype)

    def swap(array, k):
        return lax.ppermute(array, "replica", [(i, i ^ k) for i in range(PAIRED)])

    def mirror(array, k):
        return lax.ppermute(array, "tensor", [(i, i ^ k) for i in range(TENSORS)])

    def cost(bytes_accessed, flops=0):
        return pl.CostEstimate(flops=flops, bytes_accessed=bytes_accessed, transcendentals=0)

    size_a, size_b = 2 * math.prod(unit_a), 2 * math.prod(unit_b)

    plan = (arrival_adapter.T, hot_holder, hot_dest.T)
    leave = (arrival_from.T, arrival_slot.T)

    z, u, b_all, k1, k2, k3 = pl.pallas_call(
        functools.partial(pack_kernel, spans, slots),
        out_shape=(
            shaped(*unit_a), shaped(COPIES - 1, *unit_a), shaped(COPIES, *unit_b),
            shaped(*unit_k), shaped(*unit_k), shaped(*unit_k),
        ),
        in_specs=[ANY] * 7,
        out_specs=(ANY,) * 6,
        scratch_shapes=[pltpu.SMEM(x.shape, x.dtype) for x in leave + plan[:2]]
        + [
            pltpu.VMEM((COPIES,) + unit_a, kind),
            pltpu.VMEM((COPIES,) + unit_b, kind),
            pltpu.VMEM((3,) + unit_k, kind),
            pltpu.SemaphoreType.DMA((4,)),
            pltpu.SemaphoreType.DMA((2 * (2 * COPIES + 3),)),
        ],
        cost_estimate=cost(8 * size_a + 8 * size_b),
    )(*leave, *plan[:2], store_a, store_b, kv_cache)
    z2 = swap(z, 2)
    core_u, core_b = swap(u, 1), swap(b_all, 1)
    far = (swap(k2, 2), swap(k3, 3))

    u, hidden = lax.optimization_barrier((u, hidden))
    own_adapter = lax.dynamic_slice_in_dim(resident_adapter, me * resident, resident)
    every = jnp.einsum("msd,epkd->msepk", hidden[:resident], store_a, preferred_element_type=jnp.float32)
    is_own = own_adapter[:, None] == jnp.arange(slots, dtype=jnp.int32)[None, :]
    part_own = jnp.sum(jnp.where(is_own[:, None, :, None, None], every, 0.0), axis=2)
    part_own, core_u = lax.optimization_barrier((part_own, core_u))

    def pick(places, copies, core):
        out = pl.pallas_call(
            functools.partial(pick_kernel, spans, slots, places, copies),
            out_shape=tuple(shaped(*unit_a) for _ in places) + (shaped(COPIES, *unit_b),) * (copies > 0),
            in_specs=[SMEM] * 3 + [ANY] * 4,
            out_specs=(ANY,) * (len(places) + (copies > 0)),
            scratch_shapes=[
                pltpu.VMEM((len(places),) + unit_a, kind),
                pltpu.VMEM((COPIES,) + unit_b, kind),
                pltpu.SemaphoreType.DMA((2 * (len(places) + copies),)),
            ],
            cost_estimate=cost(2 * len(places) * size_a + 2 * copies * size_b),
        )(*plan, store_a, store_b, core, core_b)
        return out

    to0, to1, to2, to_b = pick((0, 1, 2), COPIES, core_u)
    f0 = swap(to0, 2)

    z2, far, to1, to_b = lax.optimization_barrier((z2, far, to1, to_b))
    f1, far_b = swap(to1, 2), swap(to_b, 2)

    _, hidden, lengths, queries, k1, kv_cache, arrival_from, arrival_slot, own_adapter = lax.optimization_barrier(
        (to0, hidden, lengths, queries, k1, kv_cache, arrival_from, arrival_slot, own_adapter)
    )
    other = mirror(hidden, 2)
    near = swap(k1, 1)

    def total(part):
        out = part
        for k in (2, 1):
            out = out + mirror(out, k)
        return out.astype(jnp.bfloat16)

    high, low = tensor_index >= 2, tensor_index % 2 == 1
    halves = jnp.concatenate([jnp.where(high, other, hidden), jnp.where(high, hidden, other)], axis=2)
    other = mirror(halves, 1)
    even, odd = jnp.where(low, other, halves), jnp.where(low, halves, other)
    whole = jnp.concatenate([even[..., :width], odd[..., :width], even[..., width:], odd[..., width:]], axis=2)
    base = jnp.einsum("msd,dgc->msgc", whole, w_kv, preferred_element_type=jnp.float32)
    f0, base, to2, z, z2 = lax.optimization_barrier((f0, base, to2, z, z2))
    f2 = swap(to2, 2)
    z1, z3 = swap(z, 1), swap(z2, 1)

    my_from = lax.dynamic_index_in_dim(arrival_from, me, 0, keepdims=False)
    my_slot = lax.dynamic_index_in_dim(arrival_slot, me, 0, keepdims=False)
    own_ids = me * resident + jnp.arange(resident, dtype=jnp.int32)
    leaving = (arrival_from * resident + arrival_slot).reshape(-1)
    staying = jnp.logical_not(jnp.any(own_ids[:, None] == leaving[None, :], axis=1))
    own_len = lax.dynamic_slice_in_dim(lengths, me * resident, resident)
    arrival_len = jnp.take(lengths, my_from * resident + my_slot)

    def fresh_rows(base_rows, shrink, up, seen):
        count = base_rows.shape[0]
        update = jnp.einsum("gnot,gote->gnoe", shrink, up, preferred_element_type=jnp.float32)
        update = update.reshape(count, steps, 2, heads, head_length).transpose(0, 1, 3, 2, 4)
        raw = base_rows + ADAPTER_SCALE * update.reshape(count, steps, heads, 2 * head_length)
        positions = seen[:, None] + jnp.arange(steps, dtype=jnp.int32)[None, :]
        turned = rotate_keys(raw[..., :head_length], positions)
        return jnp.concatenate([turned, raw[..., head_length:]], axis=-1).astype(jnp.bfloat16)

    up_own = jnp.take(store_b, own_adapter, axis=0)

    way = (my_from ^ me)[:, None, None, None]
    arrived = jnp.where(way == 1, near[None], jnp.where(way == 2, far[0][None], far[1][None]))
    row_ids = jnp.arange(kv_cache.shape[1], dtype=jnp.int32)
    arrived = jnp.where((row_ids[None, :] < arrival_len[:, None])[:, :, None, None], arrived, jnp.zeros((), jnp.bfloat16))
    rows = 16
    guests = jnp.pad(hidden[resident:].reshape(arrive * steps, width), ((0, rows - arrive * steps), (0, 0)))
    part_new, up_new = pl.pallas_call(
        functools.partial(arrive_kernel, spans, slots),
        out_shape=(shaped(arrive, rows, math.prod(unit_a[:2]), dtype=jnp.float32), shaped(arrive, *unit_b)),
        in_specs=[SMEM] * 3 + [VMEM] + [ANY] * 8,
        out_specs=(VMEM, VMEM),
        scratch_shapes=[pltpu.VMEM((arrive,) + unit_a, kind), pltpu.SemaphoreType.DMA((2 * arrive,))],
        cost_estimate=cost(arrive * (size_a + 2 * size_b), 2 * arrive * rows * size_a // 2),
    )(*plan, guests, z1, z2, z3, core_u, f0, f1, core_b, far_b)
    part = jnp.concatenate(
        [part_own.reshape(resident * steps, -1)]
        + [part_new[a, a * steps : (a + 1) * steps] for a in range(arrive)],
        axis=0,
    )
    shrink = total(part).reshape(requests, steps, 2, -1)

    seen = jnp.concatenate([own_len, arrival_len])
    live = jnp.concatenate([staying, jnp.ones((arrive,), bool)])
    fresh = fresh_rows(base, shrink, jnp.concatenate([up_own, up_new]), seen)
    mixed = attend(queries, jnp.concatenate([kv_cache, arrived]), seen, fresh)
    attn_out = jnp.where(live[:, None, None], mixed, 0.0).astype(jnp.bfloat16)
    new_kv = jnp.where(live[:, None, None, None], fresh, jnp.zeros((), jnp.bfloat16))
    installed_a, installed_b = pl.pallas_call(
        functools.partial(install_kernel, spans, slots),
        out_shape=(shaped(COPIES, *unit_a), shaped(COPIES, *unit_b)),
        in_specs=[SMEM] * 3 + [ANY] * 9,
        out_specs=(ANY, ANY),
        scratch_shapes=[
            pltpu.VMEM((COPIES,) + unit_a, kind),
            pltpu.VMEM((COPIES,) + unit_b, kind),
            pltpu.SemaphoreType.DMA((4 * COPIES,)),
        ],
        cost_estimate=cost(8 * size_a + 8 * size_b),
    )(*plan, z1, z2, z3, core_u, f0, f1, f2, core_b, far_b)
    return (attn_out, new_kv, arrived, installed_a, installed_b)


def solution(mesh):
    in_specs = (
        P(("parts", "replica"), None, "tensor"),
        P(("parts", "replica"), None, "tensor", None),
        P(("parts", "replica"), None, "tensor", None),
        P(None, "tensor", None),
        P(("parts", "replica"), None, None, "tensor"),
        P(("parts", "replica"), None, None, "tensor"),
        P("parts"),
        P("parts", None),
        P("parts", None),
        P("parts"),
        P("parts", None),
        P("parts"),
        P("parts", None),
    )
    out_specs = (
        P(("parts", "replica"), None, "tensor"),
        P(("parts", "replica"), None, "tensor", None),
        P(("parts", "replica"), None, "tensor", None),
        P(("parts", "replica"), None, None, "tensor"),
        P(("parts", "replica"), None, None, "tensor"),
    )
    local = paired if mesh.shape["replica"] == PAIRED and mesh.shape["tensor"] == TENSORS else general
    return jax.shard_map(local, mesh=mesh, in_specs=in_specs, out_specs=out_specs, check_vma=False)
```
